32 devices in a mesh: inline: 8 (over z, x), xline: 4 (over y, core).
Axes of the slice: x: 2, y: 2, z: 4, core: 2. Of those that a mesh axis runs over, the one named last changes fastest.
Arguments:
- traces: bfloat16 [8192, 2048], P(('inline', 'xline')), may hold values from -6 to 6
- trace_dest: int32 [8192, 1], P(('inline', 'xline')), may hold values from 0 to 31; in each aligned block of 256 rows (0 to 255, 256 to 511, ...) at most 16 rows name the same one
- trace_bin: int32 [8192], P(('inline', 'xline')), may hold values from 0 to 3
- trace_class: int32 [8192], P(('inline', 'xline')), may hold values from 0 to 7
- band_weights: bfloat16 [8, 16, 2, 128, 128], replicated, may hold values from -0.375 to 0.375
- conv_first: bfloat16 [32, 8, 3, 3, 3], replicated, may hold values from -0.4375 to 0.4375
- conv_second: bfloat16 [32, 32, 3, 3, 3], replicated, may hold values from -0.21875 to 0.21875
Outputs:
- regular: bfloat16 [32, 16, 8, 2048], P(None, 'inline', 'xline')
The draws below stay inside these ranges and needn't reach their ends.
Inputs may be any that keep to these rules, and one draw needn't show every extreme that they name: `trace_dest`: among the 256 traces of one device no tile is named more than 16 times, a bound that some block reaches.
All inputs are finite; a program needn't handle non-finite values.
Results may differ from the reference program's by a relative error of at most 0.0065.
Values may be sent and summed in bfloat16 or wider, within the bound.
A program may use at most 256 MiB of HBM per device.

```python
import math
import jax
import jax.numpy as jnp
import numpy as np
from jax import lax

NS = 2048
CH = 32
CLASSES = 8
BAND = 128
BI = 2
BX = 2
TR_DEV = 256
CAP = 16
NB = 16
TRACES = 8192
INLINE_BINS = 16
XLINE_BINS = 8
N_XLINE = 4
DEVICES = 32


def place_ends(array, rng, least, high):
    index_at = [jax.random.randint(jax.random.fold_in(rng, axis), (), 0, length) for axis, length in enumerate(array.shape)]
    widest = array.shape.index(max(array.shape))
    neighbour = index_at[:widest] + [(index_at[widest] + 1) % array.shape[widest]] + index_at[widest + 1:]
    return array.at[tuple(index_at)].set(least).at[tuple(neighbour)].set(high)


def shard_levels(own_key, dims, cuts, smallest, largest):
    gain = 1.0
    for position, parts in cuts:
        steps = jax.random.uniform(jax.random.fold_in(jax.random.fold_in(own_key, 6), position), (parts,), jnp.float32, smallest / len(cuts), largest / len(cuts))
        gain = gain * jnp.repeat(jnp.exp(steps), dims[position] // parts).reshape((-1,) + (1,) * (len(dims) - 1 - position))
    return gain


def assign_block(key, own, number, rows, count, top, most, lean):
    order = jax.random.permutation(key, count)
    crowded, ordinary = shares(count, rows * top, most, lean, True), shares(count, rows * top, most, lean, False)
    places = jnp.arange(count)

    def named(tallies, offset_by):
        used = int((tallies > 0).sum())
        fixed = max(1, used // 4)
        passed = fixed + (places - fixed + offset_by * (used - fixed)) % max(1, count - fixed)
        return jnp.zeros((count,), jnp.int32).at[order[jnp.where(places < fixed, places, passed)]].set(jnp.asarray(tallies, jnp.int32))

    tallies = jnp.where(number % 4 == 0, named(crowded, number // 4), named(ordinary, number - number // 4 - 1))
    mixed = jax.random.permutation(jax.random.fold_in(own, 3), count)
    source_of, receiver = mixed[0:count // 2 * 2:2], mixed[1:count // 2 * 2:2]
    slack = jnp.minimum(tallies[source_of] - 1, most - tallies[receiver]) // 2
    slack = jnp.where((source_of == order[0]) | (receiver == order[0]) | (tallies[receiver] == 0), 0, jnp.maximum(slack, 0))
    passed = jax.random.randint(jax.random.fold_in(own, 4), (count // 2,), 0, 1 << 20) % (slack + 1)
    tallies = tallies.at[source_of].add(-passed).at[receiver].add(passed)
    members = jnp.searchsorted(jnp.cumsum(tallies), jnp.arange(rows * top), side="right").astype(jnp.int32)
    table = members.reshape(top, rows).T
    table = table[jax.random.permutation(jax.random.fold_in(own, 1), rows)]
    offset_by = jax.random.randint(jax.random.fold_in(own, 2), (rows, 1), 0, top)
    return jnp.take_along_axis(table, (jnp.arange(top)[None, :] + offset_by) % top, axis=1)


def shares(amount, total, bound, skew, full):
    loads = [(1 << 20) // math.isqrt(standing ** skew) + 1 for standing in range(1, amount + 1)]
    largest = bound if full else min(bound, max(-(-total // amount), total * loads[0] // sum(loads)))
    least = 1 if total - largest >= amount - 1 else 0
    holding, surplus = [largest] + [least] * (amount - 1), total - largest - least * (amount - 1)
    while surplus > 0:
        candidates = [i for i in range(1, amount) if holding[i] < largest] or [i for i in range(1, amount) if holding[i] < bound]
        mass, remaining = sum([loads[i] for i in candidates]), surplus
        for i in candidates:
            extra = min(bound - holding[i], max(1, remaining * loads[i] // mass), surplus)
            holding[i] = holding[i] + extra
            surplus = surplus - extra
    return np.array(holding)


def noise(stream_key, shape, deviation, limit, cuts=(), dtype=jnp.bfloat16):
    gain = shard_levels(stream_key, shape, cuts, -0.22, 0.18) if cuts else 1.0
    drawn = jax.random.normal(stream_key, shape, jnp.float32) * deviation * gain
    return jnp.minimum(jnp.maximum(drawn, -limit), limit).astype(dtype)


def setup_inputs(seed: int = 0) -> dict:
    key_list = jax.random.split(jax.random.key(seed), 8)
    traces = noise(key_list[0], (TRACES, NS), 1.0, 6.0, ((0, 32),))
    trace_dest_keys = jax.random.split(jax.random.fold_in(key_list[1], 1), TRACES // TR_DEV)
    trace_dest_turns = jax.random.permutation(jax.random.fold_in(key_list[1], 3), TRACES // TR_DEV)
    trace_dest = jax.vmap(lambda own, number: assign_block(jax.random.fold_in(key_list[1], 2), own, number, TR_DEV, DEVICES, 1, CAP, 2))(trace_dest_keys, trace_dest_turns).reshape((TRACES, 1))
    trace_bin = place_ends(jax.random.randint(key_list[2], (TRACES,), 0, BI * BX), jax.random.fold_in(key_list[2], 1), 0, (BI * BX) - 1).astype(jnp.int32)
    trace_class = place_ends(jax.random.randint(key_list[3], (TRACES,), 0, CLASSES), jax.random.fold_in(key_list[3], 1), 0, CLASSES - 1).astype(jnp.int32)
    band_weights = noise(key_list[4], (CLASSES, NB, 2, BAND, BAND), (2 * BAND) ** -0.5, 0.375)
    conv_first = noise(key_list[5], (CH, CLASSES, 3, 3, 3), (27 * CLASSES) ** -0.5, 0.4375)
    conv_second = noise(key_list[6], (CH, CH, 3, 3, 3), (27 * CH) ** -0.5, 0.21875)
    return {"traces": traces, "trace_dest": trace_dest, "trace_bin": trace_bin, "trace_class": trace_class, "band_weights": band_weights, "conv_first": conv_first, "conv_second": conv_second}


def convolve(volume, kernel):
    return lax.conv_general_dilated(volume[None].astype(jnp.float32), kernel.astype(jnp.float32), (1, 1, 1), "SAME", dimension_numbers=("NCDHW", "OIDHW", "NCDHW"))[0]


def reference(traces, trace_dest, trace_bin, trace_class, band_weights, conv_first, conv_second):
    target = trace_dest[:, 0]
    inline_bin = (target // N_XLINE) * BI + trace_bin // BX
    xline_bin = (target % N_XLINE) * BX + trace_bin % BX
    segment = ((trace_class * INLINE_BINS + inline_bin) * XLINE_BINS + xline_bin).astype(jnp.int32)
    total = CLASSES * INLINE_BINS * XLINE_BINS
    stacked = jax.ops.segment_sum(traces.astype(jnp.float32), segment, num_segments=total)
    fold_count = jax.ops.segment_sum(jnp.ones(segment.shape, jnp.float32), segment, num_segments=total)
    averaged = (stacked / jnp.maximum(fold_count, 1.0)[:, None]).astype(jnp.bfloat16)
    blocks = averaged.reshape(CLASSES, INLINE_BINS * XLINE_BINS, NB, BAND).astype(jnp.float32)
    following = jnp.concatenate([blocks[:, :, 1:], jnp.zeros_like(blocks[:, :, :1])], axis=2)
    band_f = band_weights.astype(jnp.float32)
    shifted = jnp.einsum("cbkt,cktu->cbku", blocks, band_f[:, :, 0]) + jnp.einsum("cbkt,cktu->cbku", following, band_f[:, :, 1])
    volume = shifted.astype(jnp.bfloat16).reshape(CLASSES, INLINE_BINS, XLINE_BINS, NS)
    hidden = jax.nn.gelu(convolve(volume, conv_first)).astype(jnp.bfloat16)
    return convolve(hidden, conv_second).astype(jnp.bfloat16)
```

```python
import functools

import jax
import jax.numpy as jnp
from jax import lax
from jax.experimental import pallas as pl
from jax.experimental.pallas import tpu as pltpu
from jax.sharding import PartitionSpec as P

CLASSES = 8
BI = 2
BX = 2
GI = 2
LANES = 128
MESH = pl.DeviceIdType.MESH
F32 = jnp.float32
BF16 = jnp.bfloat16


def gelu(x):
    return 0.5 * x * (1.0 + jnp.tanh(0.7978845608028654 * (x + 0.044715 * (x * x * x))))


def kernel(
    planes, xsize, rows, samples, ch,
    traces, codes, band, k1, k2, out,
    rx, crx, oh, own, cown, txz, rz, ctx, crz, avg, anx, wts, vol, nxt, prv, v3, h3, t1, t2, outb,
    w_sem, l_sem, o_sem, a_send, a_recv, c_send, c_recv, z_send, z_recv, n_send, n_recv,
    e_send, e_recv, g_send, g_recv, y_send, y_recv,
):
    T = GI * xsize
    R = planes
    S = samples // T
    NCH = S // LANES
    I = GI * BI
    XL = xsize * BX
    CELLS = CLASSES * I * XL
    VR = CLASSES * XL
    HR = ch * XL
    inline = lax.axis_index("inline")
    xline = lax.axis_index("xline")
    z = lax.div(inline, GI)
    t = lax.rem(inline, GI) * xsize + xline

    def dev(zz, tt):
        return (zz * GI + lax.div(tt, xsize), lax.rem(tt, xsize))

    def mate(d):
        return lax.rem(t + d + T, T)

    def plane(d):
        return lax.rem(z + d + R, R)

    def remote(src, dst, ssem, rsem, target):
        return pltpu.make_async_remote_copy(
            src_ref=src, dst_ref=dst, send_sem=ssem, recv_sem=rsem,
            device_id=target, device_id_type=MESH,
        )

    weights = pltpu.make_async_copy(band.at[:, pl.ds(t * NCH, NCH)], wts, w_sem)
    local = []
    for c in range(NCH):
        col = pl.multiple_of(t * S + c * LANES, LANES)
        local.append(pltpu.make_async_copy(traces.at[:, pl.ds(col, LANES)], rx.at[c, 0], l_sem.at[c]))
    for copy in local:
        copy.start()
    weights.start()

    barrier = pltpu.get_barrier_semaphore()
    partners = [dev(z, mate(d)) for d in range(1, T)]
    partners += [dev(plane(d), t) for d in range(1, R)]
    partners += [dev(plane(dz), mate(dt)) for dz in (-1, 1) for dt in (-1, 1)]
    for p in partners:
        pl.semaphore_signal(barrier, inc=1, device_id=p, device_id_type=MESH)
    pl.semaphore_wait(barrier, len(partners))

    send_c, send_a = {}, {}
    for d in range(1, T):
        send_c[d] = remote(codes, crx.at[d], c_send.at[d], c_recv.at[d], dev(z, mate(d)))
        send_c[d].start()
    for c in range(NCH):
        for d in range(1, T):
            col = pl.multiple_of(mate(d) * S + c * LANES, LANES)
            send_a[c, d] = remote(
                traces.at[:, pl.ds(col, LANES)], rx.at[c, d],
                a_send.at[c * T + d], a_recv.at[c * T + d], dev(z, mate(d)),
            )
            send_a[c, d].start()

    def banded(pieces, lane_x, x):
        low, mid, high = pieces
        zero = jnp.zeros_like(mid)
        return jnp.where(
            lane_x == x - 1, low, jnp.where(lane_x == x, mid, jnp.where(lane_x == x + 1, high, zero))
        )

    q1 = 9 * CLASSES
    spread = (
        lax.div(lax.broadcasted_iota(jnp.int32, (q1, q1 * XL), 1), XL)
        == lax.broadcasted_iota(jnp.int32, (q1, q1 * XL), 0)
    ).astype(F32).astype(BF16)
    tiles = jnp.dot(k1[...], spread, preferred_element_type=F32)
    lane_x = lax.rem(lax.broadcasted_iota(jnp.int32, (ch, q1 * XL), 1), XL)
    pieces = [tiles[n * ch:(n + 1) * ch] for n in range(3)]
    for x in range(XL):
        t1[x * ch:(x + 1) * ch, :] = banded(pieces, lane_x, x).astype(BF16)

    spread = (
        lax.rem(lax.broadcasted_iota(jnp.int32, (ch, HR), 1), ch)
        == lax.broadcasted_iota(jnp.int32, (ch, HR), 0)
    ).astype(F32).astype(BF16)
    lane_x = lax.div(lax.broadcasted_iota(jnp.int32, (ch, HR), 1), ch)
    for q in range(9):
        tiles = jnp.dot(k2[q], spread, preferred_element_type=F32)
        pieces = [tiles[n * ch:(n + 1) * ch] for n in range(3)]
        for x in range(XL):
            t2[x * ch:(x + 1) * ch, q * HR:(q + 1) * HR] = banded(pieces, lane_x, x).astype(BF16)

    @pl.when(z == 0)
    def _():
        for ref in (vol, nxt, prv):
            ref[0:2] = jnp.zeros((2,) + ref.shape[1:], BF16)

    @pl.when(z == R - 1)
    def _():
        for ref in (vol, nxt, prv):
            ref[I + 2:I + 4] = jnp.zeros((2,) + ref.shape[1:], BF16)

    @pl.when(t == 0)
    def _():
        prv[...] = jnp.zeros(prv.shape, BF16)

    @pl.when(t == T - 1)
    def _():
        nxt[...] = jnp.zeros(nxt.shape, BF16)
        anx[...] = jnp.zeros(anx.shape, BF16)

    send_z, send_n = {}, {}
    for c in range(NCH):
        local[c].wait()
        for d in range(1, T):
            if c == 0:
                send_c[d].wait_recv()
            send_a[c, d].wait_recv()
        data = rx[c].reshape(T * rows, LANES)
        for d in list(range(1, R)) + [0]:
            slot = d if NCH > 1 else 0
            if c == 0:
                base = plane(d) * CELLS
                cell = lax.broadcasted_iota(jnp.int32, (CELLS, rows), 0) + base
                for s in range(T):
                    row = codes[0:1, :] if s == 0 else crx[s, 0:1, :]
                    oh[slot, :, s * rows:(s + 1) * rows] = jnp.where(cell == row, 1.0, 0.0).astype(BF16)
            total = jnp.dot(oh[slot], data, preferred_element_type=F32)
            if d == 0:
                own[c] = total
            else:
                txz[c, d] = total.astype(BF16)
                send_z[c, d] = remote(
                    txz.at[c, d], rz.at[c, d], z_send.at[c * R + d], z_recv.at[c * R + d], dev(plane(d), t)
                )
                send_z[c, d].start()
            if c == 0:
                count = lax.dot_general(
                    jnp.ones((8, T * rows), BF16), oh[slot], (((1,), (1,)), ((), ())),
                    preferred_element_type=F32,
                )
                if d == 0:
                    cown[...] = count
                else:
                    ctx[d] = count
                    send_n[d] = remote(ctx.at[d], crz.at[d], n_send.at[d], n_recv.at[d], dev(plane(d), t))
                    send_n[d].start()

    count = cown[...]
    for d in range(1, R):
        send_n[d].wait_recv()
        count = count + crz[d]
    fold = jnp.transpose(jnp.broadcast_to(jnp.maximum(count[0:1], 1.0), (LANES, CELLS)))
    to_before = remote(avg.at[0], anx, e_send, e_recv, dev(z, mate(-1)))
    for c in range(NCH):
        total = own[c]
        for d in range(1, R):
            send_z[c, d].wait_recv()
            total = total + rz[c, d].astype(F32)
        avg[c] = (total / fold).astype(BF16)
        if c == 0:
            @pl.when(t > 0)
            def _():
                to_before.start()

    weights.wait()
    for k in range(NCH - 1):
        moveout(avg[k], avg[k + 1], wts, vol, k, I, XL)

    @pl.when(t < T - 1)
    def _():
        to_before.wait_recv()

    moveout(avg[NCH - 1], anx[...], wts, vol, NCH - 1, I, XL)

    def border(dz, dt):
        here, there = {0: ((2, I), (2, I)), 1: ((I, 2), (0, 2)), -1: ((2, 2), (I + 2, 2))}[dz]
        src = vol.at[pl.ds(*here)]
        if dt == 0:
            dst = vol.at[pl.ds(*there)]
        elif dt == -1:
            src = src.at[:, :, pl.ds(0, LANES)]
            dst = nxt.at[pl.ds(*there)]
        else:
            src = src.at[:, :, pl.ds(S - LANES, LANES)]
            dst = prv.at[pl.ds(*there)]
        index = (dz + 1) * 3 + dt + 1
        return remote(src, dst, g_send.at[index], g_recv.at[index], dev(plane(dz), mate(dt)))

    def inside(dz, dt):
        return (z + dz >= 0) & (z + dz < R) & (t + dt >= 0) & (t + dt < T)

    ways = [(dz, dt) for dz in (-1, 1, 0) for dt in (-1, 0, 1) if (dz, dt) != (0, 0)]
    for dz, dt in ways:
        @pl.when(inside(dz, dt))
        def _(dz=dz, dt=dt):
            border(dz, dt).start()
    for dz, dt in ways:
        @pl.when(inside(-dz, -dt))
        def _(dz=dz, dt=dt):
            border(dz, dt).wait_recv()

    width = S + LANES
    half = lax.broadcasted_iota(jnp.int32, (VR, LANES), 1) < LANES // 2
    for r in range(I + 4):
        edge = jnp.where(half, nxt[r].astype(F32), prv[r].astype(F32))
        full = jnp.concatenate([vol[r].astype(F32), edge], axis=1)
        v3[r, 0:VR] = pltpu.roll(full, 1, 1).astype(BF16)
        v3[r, VR:2 * VR] = full.astype(BF16)
        v3[r, 2 * VR:3 * VR] = pltpu.roll(full, width - 1, 1).astype(BF16)
    lane = lax.broadcasted_iota(jnp.int32, (HR, width), 1)
    keep = (lane < S) | ((lane < S + LANES // 2) & (t < T - 1)) | ((lane >= S + LANES // 2) & (t > 0))
    for r in range(I + 2):
        total = jnp.dot(t1[...], v3[r:r + 3].reshape(9 * VR, width), preferred_element_type=F32)
        used = keep
        if r == 0:
            used = keep & (z > 0)
        if r == I + 1:
            used = keep & (z < R - 1)
        value = jnp.where(used, gelu(total), 0.0)
        h3[r, 0:HR] = pltpu.roll(value, 1, 1)[:, :S].astype(BF16)
        h3[r, HR:2 * HR] = value[:, :S].astype(BF16)
        h3[r, 2 * HR:3 * HR] = pltpu.roll(value, width - 1, 1)[:, :S].astype(BF16)

    for r in range(I):
        total = jnp.dot(t2[...], h3[r:r + 3].reshape(9 * HR, S), preferred_element_type=F32)
        outb[r] = total.astype(BF16).reshape(XL, ch, S)

    def tile(d):
        tt = mate(d)
        return outb.at[pl.ds(lax.div(tt, xsize) * BI, BI), pl.ds(lax.rem(tt, xsize) * BX, BX)]

    spot = out.at[:, :, :, pl.ds(pl.multiple_of(t * S, LANES), S)]
    send_y = {}
    for d in range(1, T):
        send_y[d] = remote(tile(d), spot, y_send.at[d], y_recv.at[d], dev(z, mate(d)))
        send_y[d].start()
    keep_own = pltpu.make_async_copy(tile(0), spot, o_sem)
    keep_own.start()
    keep_own.wait()
    for d in range(1, T):
        came = mate(-d)
        arrived = out.at[:, :, :, pl.ds(pl.multiple_of(came * S, LANES), S)]
        remote(tile(d), arrived, y_send.at[d], y_recv.at[d], dev(z, mate(d))).wait_recv()

    for copy in (send_c, send_a, send_z, send_n, send_y):
        for item in copy.values():
            item.wait_send()

    @pl.when(t > 0)
    def _():
        to_before.wait_send()

    for dz, dt in ways:
        @pl.when(inside(dz, dt))
        def _(dz=dz, dt=dt):
            border(dz, dt).wait_send()


def moveout(block, following, wts, vol, k, I, XL):
    bins = I * XL
    moved = []
    for c in range(CLASSES):
        both = jnp.concatenate(
            [block[c * bins:(c + 1) * bins], following[c * bins:(c + 1) * bins]], axis=1
        )
        moved.append(jnp.dot(both, wts[c, k], preferred_element_type=F32))
    for i in range(I):
        rows = jnp.concatenate([m[i * XL:(i + 1) * XL] for m in moved], axis=0)
        vol[2 + i, :, k * LANES:(k + 1) * LANES] = rows.astype(BF16)


def per_device(traces, trace_dest, trace_bin, trace_class, band_weights, conv_first, conv_second):
    inline_size = lax.axis_size("inline")
    xsize = lax.axis_size("xline")
    planes = inline_size // GI
    rows, samples = traces.shape
    ch = conv_first.shape[0]
    T = GI * xsize
    R = planes
    S = samples // T
    NCH = S // LANES
    I = GI * BI
    XL = xsize * BX
    CELLS = CLASSES * I * XL
    VR = CLASSES * XL
    HR = ch * XL
    nb, bw = band_weights.shape[1], band_weights.shape[-1]

    target = trace_dest.reshape(rows)
    dest_i, dest_x = target // xsize, target % xsize
    inner = (dest_i % GI) * BI + trace_bin // BX
    across = dest_x * BX + trace_bin % BX
    code = (dest_i // GI) * CELLS + (trace_class * I + inner) * XL + across
    codes = jnp.broadcast_to(code[None, :], (8, rows))
    band = band_weights.reshape(CLASSES, nb, 2 * bw, bw)
    k1 = jnp.transpose(conv_first, (3, 0, 2, 4, 1)).reshape(3 * ch, 9 * CLASSES)
    k2 = jnp.transpose(conv_second, (2, 4, 3, 0, 1)).reshape(9, 3 * ch, ch)

    vmem = pl.BlockSpec(memory_space=pltpu.VMEM)
    anyspace = pl.BlockSpec(memory_space=pl.ANY)
    dma = pltpu.SemaphoreType.DMA
    out = pl.pallas_call(
        functools.partial(kernel, planes, xsize, rows, samples, ch),
        out_shape=jax.ShapeDtypeStruct((BI, BX, ch, samples), BF16),
        in_specs=[anyspace, vmem, anyspace, vmem, vmem],
        out_specs=vmem,
        scratch_shapes=[
            pltpu.VMEM((NCH, T, rows, LANES), BF16),
            pltpu.VMEM((T, 8, rows), jnp.int32),
            pltpu.VMEM((R if NCH > 1 else 1, CELLS, T * rows), BF16),
            pltpu.VMEM((NCH, CELLS, LANES), F32),
            pltpu.VMEM((8, CELLS), F32),
            pltpu.VMEM((NCH, R, CELLS, LANES), BF16),
            pltpu.VMEM((NCH, R, CELLS, LANES), BF16),
            pltpu.VMEM((R, 8, CELLS), F32),
            pltpu.VMEM((R, 8, CELLS), F32),
            pltpu.VMEM((NCH, CELLS, LANES), BF16),
            pltpu.VMEM((CELLS, LANES), BF16),
            pltpu.VMEM((CLASSES, NCH, 2 * bw, bw), BF16),
            pltpu.VMEM((I + 4, VR, S), BF16),
            pltpu.VMEM((I + 4, VR, LANES), BF16),
            pltpu.VMEM((I + 4, VR, LANES), BF16),
            pltpu.VMEM((I + 4, 3 * VR, S + LANES), BF16),
            pltpu.VMEM((I + 2, 3 * HR, S), BF16),
            pltpu.VMEM((HR, 9 * VR), BF16),
            pltpu.VMEM((HR, 9 * HR), BF16),
            pltpu.VMEM((I, XL, ch, S), BF16),
            dma, dma((NCH,)), dma,
            dma((NCH * T,)), dma((NCH * T,)),
            dma((T,)), dma((T,)),
            dma((NCH * R,)), dma((NCH * R,)),
            dma((R,)), dma((R,)),
            dma, dma,
            dma((9,)), dma((9,)),
            dma((T,)), dma((T,)),
        ],
        compiler_params=pltpu.CompilerParams(
            collective_id=0, has_side_effects=True, vmem_limit_bytes=50 * 1024 * 1024
        ),
        name="regularize",
    )(traces, codes, band, k1, k2)
    return jnp.transpose(out, (2, 0, 1, 3))


def solution(mesh):
    return jax.shard_map(
        per_device,
        mesh=mesh,
        in_specs=(
            P(("inline", "xline"), None),
            P(("inline", "xline"), None),
            P(("inline", "xline")),
            P(("inline", "xline")),
            P(),
            P(),
            P(),
        ),
        out_specs=P(None, "inline", "xline", None),
        check_vma=False,
    )
```

```python
import functools

import jax
import jax.numpy as jnp
from jax import lax
from jax.experimental import pallas as pl
from jax.experimental.pallas import tpu as pltpu
from jax.sharding import PartitionSpec as P

CLASSES = 8
BI = 2
BX = 2
GI = 2
LANES = 128
MESH = pl.DeviceIdType.MESH
F32 = jnp.float32
BF16 = jnp.bfloat16


def gelu(x):
    return 0.5 * x * (1.0 + jnp.tanh(0.7978845608028654 * (x + 0.044715 * (x * x * x))))


def split(value, size):
    if size & (size - 1):
        return lax.div(value, size), lax.rem(value, size)
    return value >> (size.bit_length() - 1), value & (size - 1)


def band_matrices(ch, XL, k1, k2, t1, t2):
    HR = ch * XL

    def banded(pieces, lane_x, x):
        low, mid, high = pieces
        zero = jnp.zeros_like(mid)
        return jnp.where(
            lane_x == x - 1, low, jnp.where(lane_x == x, mid, jnp.where(lane_x == x + 1, high, zero))
        )

    taps = [(di, dt) for di in range(3) for dt in range(3)]
    q1 = 9 * CLASSES
    lanes = lax.broadcasted_iota(jnp.int32, (q1, q1 * XL), 1)
    spread = jnp.where(
        split(lanes, XL)[0] == lax.broadcasted_iota(jnp.int32, (q1, q1 * XL), 0), 1.0, 0.0
    ).astype(BF16)
    pieces = []
    for dx in range(3):
        rows = jnp.concatenate([k1[di * 9 + dx * 3 + dt].astype(F32) for di, dt in taps], axis=0)
        pieces.append(
            lax.dot_general(
                rows.astype(BF16), spread, (((0,), (0,)), ((), ())), preferred_element_type=F32
            )
        )
    lane_x = split(lax.broadcasted_iota(jnp.int32, (ch, q1 * XL), 1), XL)[1]
    for x in range(XL):
        t1[x * ch:(x + 1) * ch, :] = banded(pieces, lane_x, x).astype(BF16)

    lane_x, lane_c = split(lax.broadcasted_iota(jnp.int32, (ch, HR), 1), ch)
    spread = jnp.where(lane_c == lax.broadcasted_iota(jnp.int32, (ch, HR), 0), 1.0, 0.0).astype(BF16)
    for q, (di, dt) in enumerate(taps):
        pieces = [
            jnp.dot(k2[di * 9 + dx * 3 + dt], spread, preferred_element_type=F32) for dx in range(3)
        ]
        for x in range(XL):
            t2[x * ch:(x + 1) * ch, q * HR:(q + 1) * HR] = banded(pieces, lane_x, x).astype(BF16)


def kernel(
    planes, xsize, rows, samples, ch,
    traces, target, bins, classes, band, k1, k2, out,
    codes, rx, crx, oh, own, cown, txz, rz, rl, ctx, crz, avg, anx, wts, vol, nxt, prv, v3, h3, t1, t2, outb,
    w_sem, l_sem, o_sem, a_send, a_recv, c_send, c_recv, z_send, z_recv, l_recv, n_send, n_recv,
    e_send, e_recv, g_send, g_recv, y_send, y_recv,
):
    T = GI * xsize
    R = planes
    S = samples // T
    NCH = S // LANES
    I = GI * BI
    XL = xsize * BX
    CELLS = CLASSES * I * XL
    VR = CLASSES * XL
    HR = ch * XL
    inline = lax.axis_index("inline")
    xline = lax.axis_index("xline")
    z = lax.div(inline, GI)
    t = lax.rem(inline, GI) * xsize + xline

    def dev(zz, tt):
        return (zz * GI + lax.div(tt, xsize), lax.rem(tt, xsize))

    def mate(d):
        return lax.rem(t + d + T, T)

    def plane(d):
        return lax.rem(z + d + R, R)

    def remote(src, dst, ssem, rsem, target):
        return pltpu.make_async_remote_copy(
            src_ref=src, dst_ref=dst, send_sem=ssem, recv_sem=rsem,
            device_id=target, device_id_type=MESH,
        )

    weights = pltpu.make_async_copy(band.at[:, pl.ds(t * NCH, NCH)], wts, w_sem)
    local = []
    for c in range(NCH):
        col = pl.multiple_of(t * S + c * LANES, LANES)
        local.append(pltpu.make_async_copy(traces.at[:, pl.ds(col, LANES)], rx.at[c, 0], l_sem.at[c]))
    for copy in local:
        copy.start()
    weights.start()

    dest_i, dest_x = split(target[...], xsize)
    dest_z, dest_a = split(dest_i, GI)
    bin_i, bin_x = split(bins[...], BX)
    code = dest_z * CELLS + (classes[...] * I + dest_a * BI + bin_i) * XL + dest_x * BX + bin_x
    codes[...] = jnp.broadcast_to(code, (8, rows))

    barrier = pltpu.get_barrier_semaphore()
    partners = [dev(z, mate(d)) for d in range(1, T)]
    partners += [dev(plane(d), t) for d in range(1, R)]
    partners += [dev(plane(dz), mate(dt)) for dz in (-1, 1) for dt in (-1, 1)]
    for p in partners:
        pl.semaphore_signal(barrier, inc=1, device_id=p, device_id_type=MESH)
    pl.semaphore_wait(barrier, len(partners))

    send_c, send_a = {}, {}
    for d in range(1, T):
        send_c[d] = remote(codes, crx.at[d], c_send.at[d], c_recv.at[d], dev(z, mate(d)))
        send_c[d].start()
    for c in range(NCH):
        for d in range(1, T):
            col = pl.multiple_of(mate(d) * S + c * LANES, LANES)
            send_a[c, d] = remote(
                traces.at[:, pl.ds(col, LANES)], rx.at[c, d],
                a_send.at[c * T + d], a_recv.at[c * T + d], dev(z, mate(d)),
            )
            send_a[c, d].start()

    @pl.when(z == 0)
    def _():
        for ref in (vol, nxt, prv):
            ref[0:2] = jnp.zeros((2,) + ref.shape[1:], BF16)

    @pl.when(z == R - 1)
    def _():
        for ref in (vol, nxt, prv):
            ref[I + 2:I + 4] = jnp.zeros((2,) + ref.shape[1:], BF16)

    @pl.when(t == 0)
    def _():
        prv[...] = jnp.zeros(prv.shape, BF16)

    @pl.when(t == T - 1)
    def _():
        nxt[...] = jnp.zeros(nxt.shape, BF16)
        anx[...] = jnp.zeros(anx.shape, BF16)

    cell = lax.broadcasted_iota(jnp.int32, (CELLS, rows), 0)
    for d in range(T):
        if d > 0:
            send_c[d].wait_recv()
        row = codes[0:1, :] if d == 0 else crx[d, 0:1, :]
        for r in range(R):
            oh[r, :, d * rows:(d + 1) * rows] = jnp.where(cell == row - r * CELLS, 1.0, 0.0).astype(BF16)

    send_z, send_n = {}, {}
    outer = (z == 0) | (z == R - 1)

    def mirror(p):
        return jnp.where(z < 2, p, 3 - p)

    def hop(c, p, dst, rsem, r):
        return remote(txz.at[c, p], dst, z_send.at[c * R + p], rsem, dev(r, t))

    def hops(c):
        return {
            (0, True): hop(c, 0, rl.at[c], l_recv.at[c], mirror(1)),
            (0, False): hop(c, 0, rz.at[c, 0], z_recv.at[c * R], mirror(2)),
            (1, True): hop(c, 1, rz.at[c, 1], z_recv.at[c * R + 1], mirror(2)),
            (1, False): hop(c, 1, rz.at[c, 1], z_recv.at[c * R + 1], mirror(0)),
            (2, True): hop(c, 2, rz.at[c, 2], z_recv.at[c * R + 2], mirror(1)),
            (3, False): hop(c, 3, rz.at[c, 3], z_recv.at[c * R + 3], mirror(3)),
        }

    for c in range(NCH):
        local[c].wait()
        for d in range(1, T):
            send_a[c, d].wait_recv()
        data = rx[c].reshape(T * rows, LANES)
        if R == 4:
            ways = hops(c)
            for p in range(4):
                r = mirror(jnp.where(outer, (3, 2, 1, 0)[p], (2, 0, 1, 3)[p]))
                total = jnp.dot(oh[r], data, preferred_element_type=F32)
                if p < 2:
                    txz[c, p] = total.astype(BF16)

                @pl.when(outer)
                def _(p=p, total=total):
                    if p == 2:
                        txz[c, p] = total.astype(BF16)
                    if p == 3:
                        own[c] = total
                    else:
                        ways[p, True].start()

                @pl.when(jnp.logical_not(outer))
                def _(p=p, total=total):
                    if p == 2:
                        own[c] = total
                    if p == 3:
                        ways[0, True].wait_recv()
                        txz[c, p] = (total + rl[c].astype(F32)).astype(BF16)
                    if p != 2:
                        ways[p, False].start()
        else:
            for d in list(range(1, R)) + [0]:
                total = jnp.dot(oh[plane(d)], data, preferred_element_type=F32)
                if d == 0:
                    own[c] = total
                else:
                    txz[c, d] = total.astype(BF16)
                    send_z[c, d] = hop(c, d, rz.at[c, d], z_recv.at[c * R + d], plane(d))
                    send_z[c, d].start()
        if c == 0:
            for d in list(range(1, R)) + [0]:
                count = lax.dot_general(
                    jnp.ones((8, T * rows), BF16), oh[plane(d)], (((1,), (1,)), ((), ())),
                    preferred_element_type=F32,
                )
                if d == 0:
                    cown[...] = count
                else:
                    ctx[d] = count
                    send_n[d] = remote(ctx.at[d], crz.at[d], n_send.at[d], n_recv.at[d], dev(plane(d), t))
                    send_n[d].start()
            band_matrices(ch, XL, k1, k2, t1, t2)

    count = cown[...]
    for d in range(1, R):
        send_n[d].wait_recv()
        count = count + crz[d]
    fold = jnp.transpose(jnp.broadcast_to(jnp.maximum(count[0:1], 1.0), (LANES, CELLS)))
    to_before = remote(avg.at[0], anx, e_send, e_recv, dev(z, mate(-1)))
    for c in range(NCH):
        if R == 4:
            ways = hops(c)

            @pl.when(outer)
            def _():
                ways[1, False].wait_recv()
                ways[3, False].wait_recv()
                own[c] = own[c] + rz[c, 1].astype(F32) + rz[c, 3].astype(F32)

            @pl.when(jnp.logical_not(outer))
            def _():
                for p in range(3):
                    ways[p, p == 2].wait_recv()
                own[c] = own[c] + rz[c, 0].astype(F32) + rz[c, 1].astype(F32) + rz[c, 2].astype(F32)

            total = own[c]
        else:
            total = own[c]
            for d in range(1, R):
                send_z[c, d].wait_recv()
                total = total + rz[c, d].astype(F32)
        avg[c] = (total / fold).astype(BF16)
        if c == 0:
            @pl.when(t > 0)
            def _():
                to_before.start()

    weights.wait()
    for k in range(NCH - 1):
        moveout(avg[k], avg[k + 1], wts, vol, k, I, XL)

    @pl.when(t < T - 1)
    def _():
        to_before.wait_recv()

    moveout(avg[NCH - 1], anx[...], wts, vol, NCH - 1, I, XL)

    def border(dz, dt):
        here, there = {0: ((2, I), (2, I)), 1: ((I, 2), (0, 2)), -1: ((2, 2), (I + 2, 2))}[dz]
        src = vol.at[pl.ds(*here)]
        if dt == 0:
            dst = vol.at[pl.ds(*there)]
        elif dt == -1:
            src = src.at[:, :, pl.ds(0, LANES)]
            dst = nxt.at[pl.ds(*there)]
        else:
            src = src.at[:, :, pl.ds(S - LANES, LANES)]
            dst = prv.at[pl.ds(*there)]
        index = (dz + 1) * 3 + dt + 1
        return remote(src, dst, g_send.at[index], g_recv.at[index], dev(plane(dz), mate(dt)))

    def inside(dz, dt):
        return (z + dz >= 0) & (z + dz < R) & (t + dt >= 0) & (t + dt < T)

    sides = [(0, -1), (0, 1), (-1, 0), (1, 0), (-1, -1), (-1, 1), (1, -1), (1, 1)]
    for dz, dt in sides:
        @pl.when(inside(dz, dt))
        def _(dz=dz, dt=dt):
            border(dz, dt).start()

    def arrive(pairs):
        for dz, dt in pairs:
            @pl.when(inside(-dz, -dt))
            def _(dz=dz, dt=dt):
                border(dz, dt).wait_recv()

    width = S + LANES
    half = lax.broadcasted_iota(jnp.int32, (VR, LANES), 1) < LANES // 2
    lane = lax.broadcasted_iota(jnp.int32, (HR, width), 1)
    keep = (lane < S) | ((lane < S + LANES // 2) & (t < T - 1)) | ((lane >= S + LANES // 2) & (t > 0))

    def spread(r):
        edge = jnp.where(half, nxt[r].astype(F32), prv[r].astype(F32))
        full = jnp.concatenate([vol[r].astype(F32), edge], axis=1)
        v3[r, 0:VR] = pltpu.roll(full, 1, 1).astype(BF16)
        v3[r, VR:2 * VR] = full.astype(BF16)
        v3[r, 2 * VR:3 * VR] = pltpu.roll(full, width - 1, 1).astype(BF16)

    def first(r):
        total = jnp.dot(t1[...], v3[pl.ds(r, 3)].reshape(9 * VR, width), preferred_element_type=F32)
        real = ((r > 0) | (z > 0)) & ((r < I + 1) | (z < R - 1))
        value = jnp.where(keep & real, gelu(total), 0.0)
        h3[r, 0:HR] = pltpu.roll(value, 1, 1)[:, :S].astype(BF16)
        h3[r, HR:2 * HR] = value[:, :S].astype(BF16)
        h3[r, 2 * HR:3 * HR] = pltpu.roll(value, width - 1, 1)[:, :S].astype(BF16)

    arrive(sides[:2])
    for r in range(2, I + 2):
        spread(r)
    for r in range(2, I):
        first(r)
    arrive(sides[2:])
    for r in (0, 1, I + 2, I + 3):
        spread(r)

    mine = lax.div(t, xsize)

    def shared(phase, k):
        a = 1 - mine if phase == 0 else mine
        b = lax.rem(xline + k, xsize)
        source = outb.at[pl.ds(a * BI, BI), pl.ds(b * BX, BX)]
        spot = out.at[:, :, :, pl.ds(pl.multiple_of(t * S, LANES), S)]
        index = phase * xsize + k
        if index == xsize:
            return pltpu.make_async_copy(source, spot, o_sem)
        return remote(source, spot, y_send.at[index], y_recv.at[index], dev(z, a * xsize + b))

    def landed(phase, k):
        a = 1 - mine if phase == 0 else mine
        b = lax.rem(xline - k + xsize, xsize)
        spot = out.at[:, :, :, pl.ds(pl.multiple_of((a * xsize + b) * S, LANES), S)]
        index = phase * xsize + k
        source = outb.at[pl.ds(a * BI, BI), pl.ds(b * BX, BX)]
        return remote(source, spot, y_send.at[index], y_recv.at[index], dev(z, a * xsize + b))

    for phase in range(2):
        a = 1 - mine if phase == 0 else mine
        for n in range(2):
            first(a * I + n)
        for n in range(BI):
            r = a * BI + n
            total = jnp.dot(t2[...], h3[pl.ds(r, 3)].reshape(9 * HR, S), preferred_element_type=F32)
            outb[r] = total.astype(BF16).reshape(XL, ch, S)
        for k in range(xsize):
            shared(phase, k).start()
    shared(1, 0).wait()
    for phase in range(2):
        for k in range(xsize):
            if (phase, k) != (1, 0):
                landed(phase, k).wait_recv()
                shared(phase, k).wait_send()

    for copy in (send_c, send_a, send_z, send_n):
        for item in copy.values():
            item.wait_send()
    if R == 4:
        for c in range(NCH):
            ways = hops(c)
            for p in range(2):
                ways[p, False].wait_send()

            @pl.when(outer)
            def _():
                ways[2, True].wait_send()

            @pl.when(jnp.logical_not(outer))
            def _():
                ways[3, False].wait_send()

    @pl.when(t > 0)
    def _():
        to_before.wait_send()

    for dz, dt in sides:
        @pl.when(inside(dz, dt))
        def _(dz=dz, dt=dt):
            border(dz, dt).wait_send()


def moveout(block, following, wts, vol, k, I, XL):
    bins = I * XL
    moved = []
    for c in range(CLASSES):
        both = jnp.concatenate(
            [block[c * bins:(c + 1) * bins], following[c * bins:(c + 1) * bins]], axis=1
        )
        moved.append(jnp.dot(both, wts[c, k], preferred_element_type=F32))
    for i in range(I):
        rows = jnp.concatenate([m[i * XL:(i + 1) * XL] for m in moved], axis=0)
        vol[2 + i, :, k * LANES:(k + 1) * LANES] = rows.astype(BF16)


def per_device(traces, trace_dest, trace_bin, trace_class, band_weights, conv_first, conv_second):
    inline_size = lax.axis_size("inline")
    xsize = lax.axis_size("xline")
    planes = inline_size // GI
    rows, samples = traces.shape
    ch = conv_first.shape[0]
    T = GI * xsize
    R = planes
    S = samples // T
    NCH = S // LANES
    I = GI * BI
    XL = xsize * BX
    CELLS = CLASSES * I * XL
    VR = CLASSES * XL
    HR = ch * XL
    nb, bw = band_weights.shape[1], band_weights.shape[-1]

    band = band_weights.reshape(CLASSES, nb, 2 * bw, bw)
    k1 = jnp.transpose(conv_first, (2, 3, 4, 1, 0)).reshape(27, CLASSES, ch)
    k2 = jnp.transpose(conv_second, (2, 3, 4, 0, 1)).reshape(27, ch, ch)

    vmem = pl.BlockSpec(memory_space=pltpu.VMEM)
    hbm = pl.BlockSpec(memory_space=pltpu.HBM)
    dma = pltpu.SemaphoreType.DMA
    out = pl.pallas_call(
        functools.partial(kernel, planes, xsize, rows, samples, ch),
        out_shape=jax.ShapeDtypeStruct((BI, BX, ch, samples), BF16),
        in_specs=[hbm, vmem, vmem, vmem, hbm, vmem, vmem],
        out_specs=vmem,
        scratch_shapes=[
            pltpu.VMEM((8, rows), jnp.int32),
            pltpu.VMEM((NCH, T, rows, LANES), BF16),
            pltpu.VMEM((T, 8, rows), jnp.int32),
            pltpu.VMEM((R, CELLS, T * rows), BF16),
            pltpu.VMEM((NCH, CELLS, LANES), F32),
            pltpu.VMEM((8, CELLS), F32),
            pltpu.VMEM((NCH, R, CELLS, LANES), BF16),
            pltpu.VMEM((NCH, R, CELLS, LANES), BF16),
            pltpu.VMEM((NCH, CELLS, LANES), BF16),
            pltpu.VMEM((R, 8, CELLS), F32),
            pltpu.VMEM((R, 8, CELLS), F32),
            pltpu.VMEM((NCH, CELLS, LANES), BF16),
            pltpu.VMEM((CELLS, LANES), BF16),
            pltpu.VMEM((CLASSES, NCH, 2 * bw, bw), BF16),
            pltpu.VMEM((I + 4, VR, S), BF16),
            pltpu.VMEM((I + 4, VR, LANES), BF16),
            pltpu.VMEM((I + 4, VR, LANES), BF16),
            pltpu.VMEM((I + 4, 3 * VR, S + LANES), BF16),
            pltpu.VMEM((I + 2, 3 * HR, S), BF16),
            pltpu.VMEM((HR, 9 * VR), BF16),
            pltpu.VMEM((HR, 9 * HR), BF16),
            pltpu.VMEM((I, XL, ch, S), BF16),
            dma, dma((NCH,)), dma,
            dma((NCH * T,)), dma((NCH * T,)),
            dma((T,)), dma((T,)),
            dma((NCH * R,)), dma((NCH * R,)), dma((NCH,)),
            dma((R,)), dma((R,)),
            dma, dma,
            dma((9,)), dma((9,)),
            dma((T,)), dma((T,)),
        ],
        compiler_params=pltpu.CompilerParams(
            collective_id=0, has_side_effects=True, vmem_limit_bytes=60 * 1024 * 1024
        ),
        name="regularize",
    )(
        traces, trace_dest.reshape(1, rows), trace_bin.reshape(1, rows), trace_class.reshape(1, rows),
        band, k1, k2,
    )
    return jnp.transpose(out, (2, 0, 1, 3))


def solution(mesh):
    return jax.shard_map(
        per_device,
        mesh=mesh,
        in_specs=(
            P(("inline", "xline"), None),
            P(("inline", "xline"), None),
            P(("inline", "xline")),
            P(("inline", "xline")),
            P(),
            P(),
            P(),
        ),
        out_specs=P(None, "inline", "xline", None),
        check_vma=False,
    )
```

```python
import functools

import jax
import jax.numpy as jnp
from jax import lax
from jax.experimental import pallas as pl
from jax.experimental.pallas import tpu as pltpu
from jax.sharding import PartitionSpec as P

CLASSES = 8
BI = 2
BX = 2
GI = 2
LANES = 128
MESH = pl.DeviceIdType.MESH
F32 = jnp.float32
BF16 = jnp.bfloat16


def gelu(x):
    return 0.5 * x * (1.0 + jnp.tanh(0.7978845608028654 * (x + 0.044715 * (x * x * x))))


def split(value, size):
    if size & (size - 1):
        return lax.div(value, size), lax.rem(value, size)
    return value >> (size.bit_length() - 1), value & (size - 1)


def band_matrices(ch, XL, k1, k2, t1, t2):
    HR = ch * XL

    def banded(pieces, lane_x, x):
        low, mid, high = pieces
        zero = jnp.zeros_like(mid)
        return jnp.where(
            lane_x == x - 1, low, jnp.where(lane_x == x, mid, jnp.where(lane_x == x + 1, high, zero))
        )

    taps = [(di, dt) for di in range(3) for dt in range(3)]
    q1 = 9 * CLASSES
    lanes = lax.broadcasted_iota(jnp.int32, (q1, q1 * XL), 1)
    spread = jnp.where(
        split(lanes, XL)[0] == lax.broadcasted_iota(jnp.int32, (q1, q1 * XL), 0), 1.0, 0.0
    ).astype(BF16)
    pieces = []
    for dx in range(3):
        rows = jnp.concatenate([k1[di * 9 + dx * 3 + dt].astype(F32) for di, dt in taps], axis=0)
        pieces.append(
            lax.dot_general(
                rows.astype(BF16), spread, (((0,), (0,)), ((), ())), preferred_element_type=F32
            )
        )
    lane_x = split(lax.broadcasted_iota(jnp.int32, (ch, q1 * XL), 1), XL)[1]
    for x in range(XL):
        t1[x * ch:(x + 1) * ch, :] = banded(pieces, lane_x, x).astype(BF16)

    lane_x, lane_c = split(lax.broadcasted_iota(jnp.int32, (ch, HR), 1), ch)
    spread = jnp.where(lane_c == lax.broadcasted_iota(jnp.int32, (ch, HR), 0), 1.0, 0.0).astype(BF16)
    for q, (di, dt) in enumerate(taps):
        pieces = [
            jnp.dot(k2[di * 9 + dx * 3 + dt], spread, preferred_element_type=F32) for dx in range(3)
        ]
        for x in range(XL):
            t2[x * ch:(x + 1) * ch, q * HR:(q + 1) * HR] = banded(pieces, lane_x, x).astype(BF16)


def kernel(
    planes, xsize, rows, samples, ch,
    traces, target, bins, classes, band, k1, k2, out,
    codes, rx, crx, oh, own, counts, txz, rz, rl, ctx, crz, avg, anx, wts, vol, nxt, prv, v3, h3, t1, t2, outb,
    w_sem, l_sem, o_sem, a_send, a_recv, c_send, c_recv, z_send, z_recv, l_recv, n_send, n_recv,
    e_send, e_recv, g_send, g_recv, y_send, y_recv,
):
    T = GI * xsize
    R = planes
    S = samples // T
    NCH = S // LANES
    I = GI * BI
    XL = xsize * BX
    CELLS = CLASSES * I * XL
    VR = CLASSES * XL
    HR = ch * XL
    inline = lax.axis_index("inline")
    xline = lax.axis_index("xline")
    z = lax.div(inline, GI)
    t = lax.rem(inline, GI) * xsize + xline

    def dev(zz, tt):
        return (zz * GI + lax.div(tt, xsize), lax.rem(tt, xsize))

    def mate(d):
        return lax.rem(t + d + T, T)

    def plane(d):
        return lax.rem(z + d + R, R)

    def remote(src, dst, ssem, rsem, target):
        return pltpu.make_async_remote_copy(
            src_ref=src, dst_ref=dst, send_sem=ssem, recv_sem=rsem,
            device_id=target, device_id_type=MESH,
        )

    weights = pltpu.make_async_copy(band.at[:, pl.ds(t * NCH, NCH)], wts, w_sem)
    local = []
    for c in range(NCH):
        col = pl.multiple_of(t * S + c * LANES, LANES)
        local.append(pltpu.make_async_copy(traces.at[:, pl.ds(col, LANES)], rx.at[c, 0], l_sem.at[c]))
    for copy in local:
        copy.start()
    weights.start()

    dest_i, dest_x = split(target[...], xsize)
    dest_z, dest_a = split(dest_i, GI)
    bin_i, bin_x = split(bins[...], BX)
    code = dest_z * CELLS + (classes[...] * I + dest_a * BI + bin_i) * XL + dest_x * BX + bin_x
    codes[...] = jnp.broadcast_to(code, (8, rows))

    barrier = pltpu.get_barrier_semaphore()
    partners = [dev(z, mate(d)) for d in range(1, T)]
    partners += [dev(plane(d), t) for d in range(1, R)]
    partners += [dev(plane(dz), mate(dt)) for dz in (-1, 1) for dt in (-1, 1)]
    for p in partners:
        pl.semaphore_signal(barrier, inc=1, device_id=p, device_id_type=MESH)
    pl.semaphore_wait(barrier, len(partners))

    send_c, send_a = {}, {}
    for d in range(1, T):
        send_c[d] = remote(codes, crx.at[d], c_send.at[d], c_recv.at[d], dev(z, mate(d)))
        send_c[d].start()
    for c in range(NCH):
        for d in range(1, T):
            col = pl.multiple_of(mate(d) * S + c * LANES, LANES)
            send_a[c, d] = remote(
                traces.at[:, pl.ds(col, LANES)], rx.at[c, d],
                a_send.at[c * T + d], a_recv.at[c * T + d], dev(z, mate(d)),
            )
            send_a[c, d].start()

    @pl.when(z == 0)
    def _():
        for ref in (vol, nxt, prv):
            ref[0:2] = jnp.zeros((2,) + ref.shape[1:], BF16)

    @pl.when(z == R - 1)
    def _():
        for ref in (vol, nxt, prv):
            ref[I + 2:I + 4] = jnp.zeros((2,) + ref.shape[1:], BF16)

    @pl.when(t == 0)
    def _():
        prv[...] = jnp.zeros(prv.shape, BF16)

    @pl.when(t == T - 1)
    def _():
        nxt[...] = jnp.zeros(nxt.shape, BF16)
        anx[...] = jnp.zeros(anx.shape, BF16)

    cell = lax.broadcasted_iota(jnp.int32, (CELLS, rows), 0)
    for d in range(T):
        if d > 0:
            send_c[d].wait_recv()
        row = codes[0:1, :] if d == 0 else crx[d, 0:1, :]
        for r in range(R):
            oh[r, :, d * rows:(d + 1) * rows] = jnp.where(cell == row - r * CELLS, 1.0, 0.0).astype(BF16)

    band_matrices(ch, XL, k1, k2, t1, t2)

    send_z, send_n = {}, {}
    outer = (z == 0) | (z == R - 1)

    def mirror(p):
        return jnp.where(z < 2, p, 3 - p)

    def hop(c, p, dst, rsem, r):
        return remote(txz.at[c, p], dst, z_send.at[c * R + p], rsem, dev(r, t))

    def hops(c):
        return {
            (0, True): hop(c, 0, rl.at[c], l_recv.at[c], mirror(1)),
            (0, False): hop(c, 0, rz.at[c, 0], z_recv.at[c * R], mirror(2)),
            (1, True): hop(c, 1, rz.at[c, 1], z_recv.at[c * R + 1], mirror(2)),
            (1, False): hop(c, 1, rz.at[c, 1], z_recv.at[c * R + 1], mirror(0)),
            (2, True): hop(c, 2, rz.at[c, 2], z_recv.at[c * R + 2], mirror(1)),
            (3, False): hop(c, 3, rz.at[c, 3], z_recv.at[c * R + 3], mirror(3)),
        }

    for c in range(NCH):
        local[c].wait()
        for d in range(1, T):
            send_a[c, d].wait_recv()
        data = rx[c].reshape(T * rows, LANES)
        if c == 0:
            data = jnp.concatenate([data, jnp.ones((T * rows, LANES), BF16)], axis=1)

        def summed(r):
            total = jnp.dot(oh[r], data, preferred_element_type=F32)
            if c == 0:
                counts[r] = total[:, LANES:]
            return total[:, :LANES]

        if R == 4:
            ways = hops(c)
            for p in range(4):
                r = mirror(jnp.where(outer, (3, 2, 1, 0)[p], (2, 0, 1, 3)[p]))
                total = summed(r)
                if p < 2:
                    txz[c, p] = total.astype(BF16)

                @pl.when(outer)
                def _(p=p, total=total):
                    if p == 2:
                        txz[c, p] = total.astype(BF16)
                    if p == 3:
                        own[c] = total
                    else:
                        ways[p, True].start()

                @pl.when(jnp.logical_not(outer))
                def _(p=p, total=total):
                    if p == 2:
                        own[c] = total
                    if p == 3:
                        ways[0, True].wait_recv()
                        txz[c, p] = (total + rl[c].astype(F32)).astype(BF16)
                    if p != 2:
                        ways[p, False].start()
        else:
            for d in list(range(1, R)) + [0]:
                total = summed(plane(d))
                if d == 0:
                    own[c] = total
                else:
                    txz[c, d] = total.astype(BF16)
                    send_z[c, d] = hop(c, d, rz.at[c, d], z_recv.at[c * R + d], plane(d))
                    send_z[c, d].start()
        if c == 0:
            for d in range(1, R):
                ctx[d] = jnp.transpose(counts[plane(d)])[0:8]
                send_n[d] = remote(ctx.at[d], crz.at[d], n_send.at[d], n_recv.at[d], dev(plane(d), t))
                send_n[d].start()

    count = jnp.zeros((8, CELLS), F32)
    for d in range(1, R):
        send_n[d].wait_recv()
        count = count + crz[d]
    fold = counts[z] + jnp.transpose(jnp.broadcast_to(count[0:1], (LANES, CELLS)))
    fold = jnp.maximum(fold, 1.0)
    to_before = remote(avg.at[0], anx, e_send, e_recv, dev(z, mate(-1)))
    for c in range(NCH):
        if R == 4:
            ways = hops(c)

            @pl.when(outer)
            def _():
                ways[1, False].wait_recv()
                ways[3, False].wait_recv()
                own[c] = own[c] + rz[c, 1].astype(F32) + rz[c, 3].astype(F32)

            @pl.when(jnp.logical_not(outer))
            def _():
                for p in range(3):
                    ways[p, p == 2].wait_recv()
                own[c] = own[c] + rz[c, 0].astype(F32) + rz[c, 1].astype(F32) + rz[c, 2].astype(F32)

            total = own[c]
        else:
            total = own[c]
            for d in range(1, R):
                send_z[c, d].wait_recv()
                total = total + rz[c, d].astype(F32)
        avg[c] = (total / fold).astype(BF16)
        if c == 0:
            @pl.when(t > 0)
            def _():
                to_before.start()

    weights.wait()
    for k in range(NCH - 1):
        moveout(avg[k], avg[k + 1], wts, vol, k, I, XL)

    @pl.when(t < T - 1)
    def _():
        to_before.wait_recv()

    moveout(avg[NCH - 1], anx[...], wts, vol, NCH - 1, I, XL)

    def border(dz, dt):
        here, there = {0: ((2, I), (2, I)), 1: ((I, 2), (0, 2)), -1: ((2, 2), (I + 2, 2))}[dz]
        src = vol.at[pl.ds(*here)]
        if dt == 0:
            dst = vol.at[pl.ds(*there)]
        elif dt == -1:
            src = src.at[:, :, pl.ds(0, LANES)]
            dst = nxt.at[pl.ds(*there)]
        else:
            src = src.at[:, :, pl.ds(S - LANES, LANES)]
            dst = prv.at[pl.ds(*there)]
        index = (dz + 1) * 3 + dt + 1
        return remote(src, dst, g_send.at[index], g_recv.at[index], dev(plane(dz), mate(dt)))

    def inside(dz, dt):
        return (z + dz >= 0) & (z + dz < R) & (t + dt >= 0) & (t + dt < T)

    sides = [(0, -1), (0, 1), (-1, 0), (1, 0), (-1, -1), (-1, 1), (1, -1), (1, 1)]
    for dz, dt in sides:
        @pl.when(inside(dz, dt))
        def _(dz=dz, dt=dt):
            border(dz, dt).start()

    def arrive(pairs):
        for dz, dt in pairs:
            @pl.when(inside(-dz, -dt))
            def _(dz=dz, dt=dt):
                border(dz, dt).wait_recv()

    width = S + LANES
    half = lax.broadcasted_iota(jnp.int32, (VR, LANES), 1) < LANES // 2
    lane = lax.broadcasted_iota(jnp.int32, (HR, width), 1)
    keep = (lane < S) | ((lane < S + LANES // 2) & (t < T - 1)) | ((lane >= S + LANES // 2) & (t > 0))

    def spread(r):
        edge = jnp.where(half, nxt[r].astype(F32), prv[r].astype(F32))
        full = jnp.concatenate([vol[r].astype(F32), edge], axis=1)
        v3[r, 0:VR] = pltpu.roll(full, 1, 1).astype(BF16)
        v3[r, VR:2 * VR] = full.astype(BF16)
        v3[r, 2 * VR:3 * VR] = pltpu.roll(full, width - 1, 1).astype(BF16)

    def first(r):
        total = jnp.dot(t1[...], v3[pl.ds(r, 3)].reshape(9 * VR, width), preferred_element_type=F32)
        real = ((r > 0) | (z > 0)) & ((r < I + 1) | (z < R - 1))
        value = jnp.where(keep & real, gelu(total), 0.0)
        h3[r, 0:HR] = pltpu.roll(value, 1, 1)[:, :S].astype(BF16)
        h3[r, HR:2 * HR] = value[:, :S].astype(BF16)
        h3[r, 2 * HR:3 * HR] = pltpu.roll(value, width - 1, 1)[:, :S].astype(BF16)

    arrive(sides[:2])
    for r in range(2, I + 2):
        spread(r)
    for r in range(2, I):
        first(r)
    arrive(sides[2:])
    for r in (0, 1, I + 2, I + 3):
        spread(r)

    mine = lax.div(t, xsize)

    def tile_row(phase, n):
        a = 1 - mine if phase == 0 else mine
        return a, a * BI + (1 - a) * (1 - n) + a * n

    def shared(phase, n, k):
        a, r = tile_row(phase, n)
        b = lax.rem(xline + k, xsize)
        source = outb.at[r, pl.ds(b * BX, BX)]
        spot = out.at[r - a * BI, :, :, pl.ds(pl.multiple_of(t * S, LANES), S)]
        index = (phase * BI + n) * xsize + k
        if phase == 1 and k == 0:
            return pltpu.make_async_copy(source, spot, o_sem.at[n])
        return remote(source, spot, y_send.at[index], y_recv.at[index], dev(z, a * xsize + b))

    def landed(phase, n, k):
        a = 1 - mine if phase == 0 else mine
        r = (1 - mine) * (1 - n) + mine * n
        b = lax.rem(xline - k + xsize, xsize)
        spot = out.at[r, :, :, pl.ds(pl.multiple_of((a * xsize + b) * S, LANES), S)]
        index = (phase * BI + n) * xsize + k
        source = outb.at[r, pl.ds(b * BX, BX)]
        return remote(source, spot, y_send.at[index], y_recv.at[index], dev(z, a * xsize + b))

    steps = [(phase, n) for phase in range(2) for n in range(BI)]
    for phase, n in steps:
        a, r = tile_row(phase, n)
        first(r + a * 2)
        total = jnp.dot(t2[...], h3[pl.ds(r, 3)].reshape(9 * HR, S), preferred_element_type=F32)
        outb[r] = total.astype(BF16).reshape(XL, ch, S)
        for k in range(xsize):
            shared(phase, n, k).start()
    for phase, n in steps:
        for k in range(xsize):
            if (phase, k) == (1, 0):
                shared(phase, n, k).wait()
            else:
                landed(phase, n, k).wait_recv()
                shared(phase, n, k).wait_send()

    for copy in (send_c, send_a, send_z, send_n):
        for item in copy.values():
            item.wait_send()
    if R == 4:
        for c in range(NCH):
            ways = hops(c)
            for p in range(2):
                ways[p, False].wait_send()

            @pl.when(outer)
            def _():
                ways[2, True].wait_send()

            @pl.when(jnp.logical_not(outer))
            def _():
                ways[3, False].wait_send()

    @pl.when(t > 0)
    def _():
        to_before.wait_send()

    for dz, dt in sides:
        @pl.when(inside(dz, dt))
        def _(dz=dz, dt=dt):
            border(dz, dt).wait_send()


def moveout(block, following, wts, vol, k, I, XL):
    bins = I * XL
    moved = []
    for c in range(CLASSES):
        both = jnp.concatenate(
            [block[c * bins:(c + 1) * bins], following[c * bins:(c + 1) * bins]], axis=1
        )
        moved.append(jnp.dot(both, wts[c, k], preferred_element_type=F32))
    for i in range(I):
        rows = jnp.concatenate([m[i * XL:(i + 1) * XL] for m in moved], axis=0)
        vol[2 + i, :, k * LANES:(k + 1) * LANES] = rows.astype(BF16)


def per_device(traces, trace_dest, trace_bin, trace_class, band_weights, conv_first, conv_second):
    inline_size = lax.axis_size("inline")
    xsize = lax.axis_size("xline")
    planes = inline_size // GI
    rows, samples = traces.shape
    ch = conv_first.shape[0]
    T = GI * xsize
    R = planes
    S = samples // T
    NCH = S // LANES
    I = GI * BI
    XL = xsize * BX
    CELLS = CLASSES * I * XL
    VR = CLASSES * XL
    HR = ch * XL
    nb, bw = band_weights.shape[1], band_weights.shape[-1]

    band = band_weights.reshape(CLASSES, nb, 2 * bw, bw)
    k1 = jnp.transpose(conv_first, (2, 3, 4, 1, 0)).reshape(27, CLASSES, ch)
    k2 = jnp.transpose(conv_second, (2, 3, 4, 0, 1)).reshape(27, ch, ch)

    vmem = pl.BlockSpec(memory_space=pltpu.VMEM)
    hbm = pl.BlockSpec(memory_space=pltpu.HBM)
    dma = pltpu.SemaphoreType.DMA
    out = pl.pallas_call(
        functools.partial(kernel, planes, xsize, rows, samples, ch),
        out_shape=jax.ShapeDtypeStruct((BI, BX, ch, samples), BF16),
        in_specs=[hbm, vmem, vmem, vmem, hbm, vmem, vmem],
        out_specs=vmem,
        scratch_shapes=[
            pltpu.VMEM((8, rows), jnp.int32),
            pltpu.VMEM((NCH, T, rows, LANES), BF16),
            pltpu.VMEM((T, 8, rows), jnp.int32),
            pltpu.VMEM((R, CELLS, T * rows), BF16),
            pltpu.VMEM((NCH, CELLS, LANES), F32),
            pltpu.VMEM((R, CELLS, LANES), F32),
            pltpu.VMEM((NCH, R, CELLS, LANES), BF16),
            pltpu.VMEM((NCH, R, CELLS, LANES), BF16),
            pltpu.VMEM((NCH, CELLS, LANES), BF16),
            pltpu.VMEM((R, 8, CELLS), F32),
            pltpu.VMEM((R, 8, CELLS), F32),
            pltpu.VMEM((NCH, CELLS, LANES), BF16),
            pltpu.VMEM((CELLS, LANES), BF16),
            pltpu.VMEM((CLASSES, NCH, 2 * bw, bw), BF16),
            pltpu.VMEM((I + 4, VR, S), BF16),
            pltpu.VMEM((I + 4, VR, LANES), BF16),
            pltpu.VMEM((I + 4, VR, LANES), BF16),
            pltpu.VMEM((I + 4, 3 * VR, S + LANES), BF16),
            pltpu.VMEM((I + 2, 3 * HR, S), BF16),
            pltpu.VMEM((HR, 9 * VR), BF16),
            pltpu.VMEM((HR, 9 * HR), BF16),
            pltpu.VMEM((I, XL, ch, S), BF16),
            dma, dma((NCH,)), dma((BI,)),
            dma((NCH * T,)), dma((NCH * T,)),
            dma((T,)), dma((T,)),
            dma((NCH * R,)), dma((NCH * R,)), dma((NCH,)),
            dma((R,)), dma((R,)),
            dma, dma,
            dma((9,)), dma((9,)),
            dma((BI * T,)), dma((BI * T,)),
        ],
        compiler_params=pltpu.CompilerParams(
            collective_id=0, has_side_effects=True, vmem_limit_bytes=(53 if T <= 8 else 60) * 1024 * 1024
        ),
        name="regularize",
    )(
        traces, trace_dest.reshape(1, rows), trace_bin.reshape(1, rows), trace_class.reshape(1, rows),
        band, k1, k2,
    )
    return jnp.transpose(out, (2, 0, 1, 3))


def solution(mesh):
    return jax.shard_map(
        per_device,
        mesh=mesh,
        in_specs=(
            P(("inline", "xline"), None),
            P(("inline", "xline"), None),
            P(("inline", "xline")),
            P(("inline", "xline")),
            P(),
            P(),
            P(),
        ),
        out_specs=P(None, "inline", "xline", None),
        check_vma=False,
    )
```

```python
import functools

import jax
import jax.numpy as jnp
from jax import lax
from jax.experimental import pallas as pl
from jax.experimental.pallas import tpu as pltpu
from jax.sharding import PartitionSpec as P

CLASSES = 8
BI = 2
BX = 2
GI = 2
LANES = 128
MESH = pl.DeviceIdType.MESH
F32 = jnp.float32
BF16 = jnp.bfloat16


def gelu(x):
    return 0.5 * x * (1.0 + jnp.tanh(0.7978845608028654 * (x + 0.044715 * (x * x * x))))


def split(value, size):
    if size & (size - 1):
        return lax.div(value, size), lax.rem(value, size)
    return value >> (size.bit_length() - 1), value & (size - 1)


def band_matrices(ch, XL, k1, k2, t1, t2):
    HR = ch * XL

    def banded(pieces, lane_x, x):
        low, mid, high = pieces
        zero = jnp.zeros_like(mid)
        return jnp.where(
            lane_x == x - 1, low, jnp.where(lane_x == x, mid, jnp.where(lane_x == x + 1, high, zero))
        )

    taps = [(di, dt) for di in range(3) for dt in range(3)]
    q1 = 9 * CLASSES
    lanes = lax.broadcasted_iota(jnp.int32, (q1, q1 * XL), 1)
    spread = jnp.where(
        split(lanes, XL)[0] == lax.broadcasted_iota(jnp.int32, (q1, q1 * XL), 0), 1.0, 0.0
    ).astype(BF16)
    pieces = []
    for dx in range(3):
        rows = jnp.concatenate([k1[di * 9 + dx * 3 + dt].astype(F32) for di, dt in taps], axis=0)
        pieces.append(
            lax.dot_general(
                rows.astype(BF16), spread, (((0,), (0,)), ((), ())), preferred_element_type=F32
            )
        )
    lane_x = split(lax.broadcasted_iota(jnp.int32, (ch, q1 * XL), 1), XL)[1]
    for x in range(XL):
        t1[x * ch:(x + 1) * ch, :] = banded(pieces, lane_x, x).astype(BF16)

    lane_x, lane_c = split(lax.broadcasted_iota(jnp.int32, (ch, HR), 1), ch)
    spread = jnp.where(lane_c == lax.broadcasted_iota(jnp.int32, (ch, HR), 0), 1.0, 0.0).astype(BF16)

    def tap(q, carry):
        first = (q // 3) * 9 + q % 3
        pieces = [jnp.dot(k2[first + dx * 3], spread, preferred_element_type=F32) for dx in range(3)]
        spot = pl.ds(pl.multiple_of(q * HR, LANES), HR)
        for x in range(XL):
            t2[x * ch:(x + 1) * ch, spot] = banded(pieces, lane_x, x).astype(BF16)
        return carry

    lax.fori_loop(0, 9, tap, 0)


def kernel(
    planes, xsize, rows, samples, ch,
    traces, target_h, bins_h, classes_h, band, k1_h, k2_h, out,
    target, bins, classes, k1, k2, codes, rx, crx, oh, own, counts, txz, rz, rl, ctx, crz, avg, anx, wts, vol, nxt, prv, v3, h3, t1, t2, outb,
    i_sem, w_sem, l_sem, o_sem, a_send, a_recv, c_send, c_recv, z_send, z_recv, l_recv, n_send, n_recv,
    e_send, e_recv, g_send, g_recv, y_send, y_recv,
):
    T = GI * xsize
    R = planes
    S = samples // T
    NCH = S // LANES
    I = GI * BI
    XL = xsize * BX
    CELLS = CLASSES * I * XL
    VR = CLASSES * XL
    HR = ch * XL
    inline = lax.axis_index("inline")
    xline = lax.axis_index("xline")
    z = lax.div(inline, GI)
    t = lax.rem(inline, GI) * xsize + xline

    def dev(zz, tt):
        return (zz * GI + lax.div(tt, xsize), lax.rem(tt, xsize))

    def mate(d):
        return lax.rem(t + d + T, T)

    def plane(d):
        return lax.rem(z + d + R, R)

    def remote(src, dst, ssem, rsem, target):
        return pltpu.make_async_remote_copy(
            src_ref=src, dst_ref=dst, send_sem=ssem, recv_sem=rsem,
            device_id=target, device_id_type=MESH,
        )

    weights = pltpu.make_async_copy(band.at[:, pl.ds(t * NCH, NCH)], wts, w_sem)
    local = []
    for c in range(NCH):
        col = pl.multiple_of(t * S + c * LANES, LANES)
        local.append(pltpu.make_async_copy(traces.at[:, pl.ds(col, LANES)], rx.at[c, 0], l_sem.at[c]))
    pairs = ((target_h, target), (bins_h, bins), (classes_h, classes), (k1_h, k1), (k2_h, k2))
    fetch = [pltpu.make_async_copy(a, b, i_sem.at[n]) for n, (a, b) in enumerate(pairs)]
    for copy in fetch:
        copy.start()

    barrier = pltpu.get_barrier_semaphore()
    partners = [dev(z, mate(d)) for d in range(1, T)]
    partners += [dev(plane(d), t) for d in range(1, R)]
    partners += [dev(plane(dz), mate(dt)) for dz in (-1, 1) for dt in (-1, 1)]
    for p in partners:
        pl.semaphore_signal(barrier, inc=1, device_id=p, device_id_type=MESH)

    for copy in fetch[:3]:
        copy.wait()
    dest_i, dest_x = split(target[...], xsize)
    dest_z, dest_a = split(dest_i, GI)
    bin_i, bin_x = split(bins[...], BX)
    code = dest_z * CELLS + (classes[...] * I + dest_a * BI + bin_i) * XL + dest_x * BX + bin_x
    codes[...] = jnp.broadcast_to(code, (8, rows))
    pl.semaphore_wait(barrier, len(partners))

    send_c, send_a = {}, {}
    for d in range(1, T):
        send_c[d] = remote(codes, crx.at[d], c_send.at[d], c_recv.at[d], dev(z, mate(d)))
        send_c[d].start()
    for c in range(NCH):
        for d in range(1, T):
            col = pl.multiple_of(mate(d) * S + c * LANES, LANES)
            send_a[c, d] = remote(
                traces.at[:, pl.ds(col, LANES)], rx.at[c, d],
                a_send.at[c * T + d], a_recv.at[c * T + d], dev(z, mate(d)),
            )
            send_a[c, d].start()
        local[c].start()
    weights.start()

    @pl.when(z == 0)
    def _():
        for ref in (vol, nxt, prv):
            ref[0:2] = jnp.zeros((2,) + ref.shape[1:], BF16)

    @pl.when(z == R - 1)
    def _():
        for ref in (vol, nxt, prv):
            ref[I + 2:I + 4] = jnp.zeros((2,) + ref.shape[1:], BF16)

    @pl.when(t == 0)
    def _():
        prv[...] = jnp.zeros(prv.shape, BF16)

    @pl.when(t == T - 1)
    def _():
        nxt[...] = jnp.zeros(nxt.shape, BF16)
        anx[...] = jnp.zeros(anx.shape, BF16)

    cell = lax.broadcasted_iota(jnp.int32, (CELLS, rows), 0)

    def one_hot(d, row):
        spot = pl.ds(pl.multiple_of(d * rows, LANES), rows)
        for r in range(R):
            oh[r, :, spot] = jnp.where(cell == row - r * CELLS, 1.0, 0.0).astype(BF16)

    def arrived_code(d, carry):
        remote(codes, crx.at[d], c_send.at[d], c_recv.at[d], dev(z, t)).wait_recv()
        one_hot(d, crx[d][0:1, :])
        return carry

    one_hot(0, codes[0:1, :])
    lax.fori_loop(1, T, arrived_code, 0)
    for copy in fetch[3:]:
        copy.wait()
    band_matrices(ch, XL, k1, k2, t1, t2)

    send_z, send_n = {}, {}
    outer = (z == 0) | (z == R - 1)

    def mirror(p):
        return jnp.where(z < 2, p, 3 - p)

    def hop(c, p, dst, rsem, r):
        return remote(txz.at[c, p], dst, z_send.at[c * R + p], rsem, dev(r, t))

    def hops(c):
        return {
            (0, True): hop(c, 0, rl.at[c], l_recv.at[c], mirror(1)),
            (0, False): hop(c, 0, rz.at[c, 0], z_recv.at[c * R], mirror(2)),
            (1, True): hop(c, 1, rz.at[c, 1], z_recv.at[c * R + 1], mirror(2)),
            (1, False): hop(c, 1, rz.at[c, 1], z_recv.at[c * R + 1], mirror(0)),
            (2, True): hop(c, 2, rz.at[c, 2], z_recv.at[c * R + 2], mirror(1)),
            (3, False): hop(c, 3, rz.at[c, 3], z_recv.at[c * R + 3], mirror(3)),
        }

    for c in range(NCH):
        local[c].wait()
        for d in range(1, T):
            send_a[c, d].wait_recv()
        data = rx[c].reshape(T * rows, LANES)
        data = jnp.concatenate([data, jnp.ones((T * rows, LANES), BF16)], axis=1)

        def summed(r):
            total = jnp.dot(oh[r], data, preferred_element_type=F32)
            if c == 0:
                counts[r] = total[:, LANES:]
            return total[:, :LANES]

        if R == 4:
            ways = hops(c)
            inner = jnp.logical_not(outer)

            def part(p, carry):
                r = mirror(jnp.where(outer, 3 - p, jnp.where(p == 0, 2, jnp.where(p == 3, 3, p - 1))))
                total = summed(r)
                txz[c, p] = total.astype(BF16)

                @pl.when((outer & (p == 3)) | (inner & (p == 2)))
                def _():
                    own[c] = total

                @pl.when(outer & (p == 0))
                def _():
                    ways[0, True].start()

                @pl.when(inner & (p == 0))
                def _():
                    ways[0, False].start()

                @pl.when(outer & (p == 1))
                def _():
                    ways[1, True].start()

                @pl.when(inner & (p == 1))
                def _():
                    ways[1, False].start()

                @pl.when(outer & (p == 2))
                def _():
                    ways[2, True].start()

                @pl.when(inner & (p == 3))
                def _():
                    ways[0, True].wait_recv()
                    txz[c, p] = (total + rl[c].astype(F32)).astype(BF16)
                    ways[3, False].start()

                return carry

            lax.fori_loop(0, 4, part, 0)
        else:
            for d in list(range(1, R)) + [0]:
                total = summed(plane(d))
                if d == 0:
                    own[c] = total
                else:
                    txz[c, d] = total.astype(BF16)
                    send_z[c, d] = hop(c, d, rz.at[c, d], z_recv.at[c * R + d], plane(d))
                    send_z[c, d].start()
        if c == 0:
            for d in range(1, R):
                ctx[d] = jnp.transpose(counts[plane(d)])[0:8]
                send_n[d] = remote(ctx.at[d], crz.at[d], n_send.at[d], n_recv.at[d], dev(plane(d), t))
                send_n[d].start()

    count = jnp.zeros((8, CELLS), F32)
    for d in range(1, R):
        send_n[d].wait_recv()
        count = count + crz[d]
    fold = counts[z] + jnp.transpose(jnp.broadcast_to(count[0:1], (LANES, CELLS)))
    fold = jnp.maximum(fold, 1.0)
    to_before = remote(avg.at[0], anx, e_send, e_recv, dev(z, mate(-1)))
    for c in range(NCH):
        if R == 4:
            ways = hops(c)

            @pl.when(outer)
            def _():
                ways[1, False].wait_recv()
                ways[3, False].wait_recv()
                own[c] = own[c] + rz[c, 1].astype(F32) + rz[c, 3].astype(F32)

            @pl.when(jnp.logical_not(outer))
            def _():
                for p in range(3):
                    ways[p, p == 2].wait_recv()
                own[c] = own[c] + rz[c, 0].astype(F32) + rz[c, 1].astype(F32) + rz[c, 2].astype(F32)

            total = own[c]
        else:
            total = own[c]
            for d in range(1, R):
                send_z[c, d].wait_recv()
                total = total + rz[c, d].astype(F32)
        avg[c] = (total / fold).astype(BF16)
        if c == 0:
            @pl.when(t > 0)
            def _():
                to_before.start()

    weights.wait()
    for k in range(NCH - 1):
        moveout(avg[k], avg[k + 1], wts, vol, k, I, XL)

    @pl.when(t < T - 1)
    def _():
        to_before.wait_recv()

    moveout(avg[NCH - 1], anx[...], wts, vol, NCH - 1, I, XL)

    def border(dz, dt):
        here, there = {0: ((2, I), (2, I)), 1: ((I, 2), (0, 2)), -1: ((2, 2), (I + 2, 2))}[dz]
        src = vol.at[pl.ds(*here)]
        if dt == 0:
            dst = vol.at[pl.ds(*there)]
        elif dt == -1:
            src = src.at[:, :, pl.ds(0, LANES)]
            dst = nxt.at[pl.ds(*there)]
        else:
            src = src.at[:, :, pl.ds(S - LANES, LANES)]
            dst = prv.at[pl.ds(*there)]
        index = (dz + 1) * 3 + dt + 1
        return remote(src, dst, g_send.at[index], g_recv.at[index], dev(plane(dz), mate(dt)))

    def inside(dz, dt):
        return (z + dz >= 0) & (z + dz < R) & (t + dt >= 0) & (t + dt < T)

    sides = [(0, -1), (0, 1), (-1, 0), (1, 0), (-1, -1), (-1, 1), (1, -1), (1, 1)]
    for dz, dt in sides:
        @pl.when(inside(dz, dt))
        def _(dz=dz, dt=dt):
            border(dz, dt).start()

    def arrive(pairs):
        for dz, dt in pairs:
            @pl.when(inside(-dz, -dt))
            def _(dz=dz, dt=dt):
                border(dz, dt).wait_recv()

    width = S + LANES
    half = lax.broadcasted_iota(jnp.int32, (VR, LANES), 1) < LANES // 2
    lane = lax.broadcasted_iota(jnp.int32, (HR, width), 1)
    keep = (lane < S) | ((lane < S + LANES // 2) & (t < T - 1)) | ((lane >= S + LANES // 2) & (t > 0))

    def spread(r):
        edge = jnp.where(half, nxt[r].astype(F32), prv[r].astype(F32))
        full = jnp.concatenate([vol[r].astype(F32), edge], axis=1)
        v3[r, 0:VR] = pltpu.roll(full, 1, 1).astype(BF16)
        v3[r, VR:2 * VR] = full.astype(BF16)
        v3[r, 2 * VR:3 * VR] = pltpu.roll(full, width - 1, 1).astype(BF16)

    def first(r):
        total = jnp.dot(t1[...], v3[pl.ds(r, 3)].reshape(9 * VR, width), preferred_element_type=F32)
        real = ((r > 0) | (z > 0)) & ((r < I + 1) | (z < R - 1))
        value = jnp.where(keep & real, gelu(total), 0.0)
        h3[r, 0:HR] = pltpu.roll(value, 1, 1)[:, :S].astype(BF16)
        h3[r, HR:2 * HR] = value[:, :S].astype(BF16)
        h3[r, 2 * HR:3 * HR] = pltpu.roll(value, width - 1, 1)[:, :S].astype(BF16)

    arrive(sides[:2])
    for r in range(2, I + 2):
        spread(r)
    for r in range(2, I):
        first(r)
    arrive(sides[2:])
    for r in (0, 1, I + 2, I + 3):
        spread(r)

    mine = lax.div(t, xsize)

    def tile_row(phase, n):
        a = 1 - mine if phase == 0 else mine
        return a, a * BI + (1 - a) * (1 - n) + a * n

    def shared(phase, n, k):
        a, r = tile_row(phase, n)
        b = lax.rem(xline + k, xsize)
        source = outb.at[r, pl.ds(b * BX, BX)]
        spot = out.at[r - a * BI, :, :, pl.ds(pl.multiple_of(t * S, LANES), S)]
        index = (phase * BI + n) * xsize + k
        if phase == 1 and k == 0:
            return pltpu.make_async_copy(source, spot, o_sem.at[n])
        return remote(source, spot, y_send.at[index], y_recv.at[index], dev(z, a * xsize + b))

    def landed(phase, n, k):
        a = 1 - mine if phase == 0 else mine
        r = (1 - mine) * (1 - n) + mine * n
        b = lax.rem(xline - k + xsize, xsize)
        spot = out.at[r, :, :, pl.ds(pl.multiple_of((a * xsize + b) * S, LANES), S)]
        index = (phase * BI + n) * xsize + k
        source = outb.at[r, pl.ds(b * BX, BX)]
        return remote(source, spot, y_send.at[index], y_recv.at[index], dev(z, a * xsize + b))

    steps = [(phase, n) for phase in range(2) for n in range(BI)]
    for phase, n in steps:
        a, r = tile_row(phase, n)
        first(r + a * 2)
        total = jnp.dot(t2[...], h3[pl.ds(r, 3)].reshape(9 * HR, S), preferred_element_type=F32)
        outb[r] = total.astype(BF16).reshape(XL, ch, S)
        for k in range(xsize):
            shared(phase, n, k).start()
    for phase, n in steps:
        for k in range(xsize):
            if (phase, k) == (1, 0):
                shared(phase, n, k).wait()
            else:
                landed(phase, n, k).wait_recv()
                shared(phase, n, k).wait_send()

    for copy in (send_c, send_a, send_z, send_n):
        for item in copy.values():
            item.wait_send()
    if R == 4:
        for c in range(NCH):
            ways = hops(c)
            for p in range(2):
                ways[p, False].wait_send()

            @pl.when(outer)
            def _():
                ways[2, True].wait_send()

            @pl.when(jnp.logical_not(outer))
            def _():
                ways[3, False].wait_send()

    @pl.when(t > 0)
    def _():
        to_before.wait_send()

    for dz, dt in sides:
        @pl.when(inside(dz, dt))
        def _(dz=dz, dt=dt):
            border(dz, dt).wait_send()


def moveout(block, following, wts, vol, k, I, XL):
    bins = I * XL
    moved = []
    for c in range(CLASSES):
        both = jnp.concatenate(
            [block[c * bins:(c + 1) * bins], following[c * bins:(c + 1) * bins]], axis=1
        )
        moved.append(jnp.dot(both, wts[c, k], preferred_element_type=F32))
    for i in range(I):
        rows = jnp.concatenate([m[i * XL:(i + 1) * XL] for m in moved], axis=0)
        vol[2 + i, :, k * LANES:(k + 1) * LANES] = rows.astype(BF16)


def per_device(traces, trace_dest, trace_bin, trace_class, band_weights, conv_first, conv_second):
    inline_size = lax.axis_size("inline")
    xsize = lax.axis_size("xline")
    planes = inline_size // GI
    rows, samples = traces.shape
    ch = conv_first.shape[0]
    T = GI * xsize
    R = planes
    S = samples // T
    NCH = S // LANES
    I = GI * BI
    XL = xsize * BX
    CELLS = CLASSES * I * XL
    VR = CLASSES * XL
    HR = ch * XL
    nb, bw = band_weights.shape[1], band_weights.shape[-1]

    band = band_weights.reshape(CLASSES, nb, 2 * bw, bw)
    k1 = jnp.transpose(conv_first, (2, 3, 4, 1, 0)).reshape(27, CLASSES, ch)
    k2 = jnp.transpose(conv_second, (2, 3, 4, 0, 1)).reshape(27, ch, ch)

    vmem = pl.BlockSpec(memory_space=pltpu.VMEM)
    hbm = pl.BlockSpec(memory_space=pltpu.HBM)
    dma = pltpu.SemaphoreType.DMA
    out = pl.pallas_call(
        functools.partial(kernel, planes, xsize, rows, samples, ch),
        out_shape=jax.ShapeDtypeStruct((BI, BX, ch, samples), BF16),
        in_specs=[hbm] * 7,
        out_specs=vmem,
        scratch_shapes=[
            pltpu.VMEM((1, rows), jnp.int32),
            pltpu.VMEM((1, rows), jnp.int32),
            pltpu.VMEM((1, rows), jnp.int32),
            pltpu.VMEM((27, CLASSES, ch), BF16),
            pltpu.VMEM((27, ch, ch), BF16),
            pltpu.VMEM((8, rows), jnp.int32),
            pltpu.VMEM((NCH, T, rows, LANES), BF16),
            pltpu.VMEM((T, 8, rows), jnp.int32),
            pltpu.VMEM((R, CELLS, T * rows), BF16),
            pltpu.VMEM((NCH, CELLS, LANES), F32),
            pltpu.VMEM((R, CELLS, LANES), F32),
            pltpu.VMEM((NCH, R, CELLS, LANES), BF16),
            pltpu.VMEM((NCH, R, CELLS, LANES), BF16),
            pltpu.VMEM((NCH, CELLS, LANES), BF16),
            pltpu.VMEM((R, 8, CELLS), F32),
            pltpu.VMEM((R, 8, CELLS), F32),
            pltpu.VMEM((NCH, CELLS, LANES), BF16),
            pltpu.VMEM((CELLS, LANES), BF16),
            pltpu.VMEM((CLASSES, NCH, 2 * bw, bw), BF16),
            pltpu.VMEM((I + 4, VR, S), BF16),
            pltpu.VMEM((I + 4, VR, LANES), BF16),
            pltpu.VMEM((I + 4, VR, LANES), BF16),
            pltpu.VMEM((I + 4, 3 * VR, S + LANES), BF16),
            pltpu.VMEM((I + 2, 3 * HR, S), BF16),
            pltpu.VMEM((HR, 9 * VR), BF16),
            pltpu.VMEM((HR, 9 * HR), BF16),
            pltpu.VMEM((I, XL, ch, S), BF16),
            dma((5,)), dma, dma((NCH,)), dma((BI,)),
            dma((NCH * T,)), dma((NCH * T,)),
            dma((T,)), dma((T,)),
            dma((NCH * R,)), dma((NCH * R,)), dma((NCH,)),
            dma((R,)), dma((R,)),
            dma, dma,
            dma((9,)), dma((9,)),
            dma((BI * T,)), dma((BI * T,)),
        ],
        compiler_params=pltpu.CompilerParams(
            collective_id=0, has_side_effects=True, vmem_limit_bytes=(61440 if T <= 8 else 60 * 1024) * 1024
        ),
        name="regularize",
    )(
        traces, trace_dest.reshape(1, rows), trace_bin.reshape(1, rows), trace_class.reshape(1, rows),
        band, k1, k2,
    )
    return jnp.transpose(out, (2, 0, 1, 3))


def solution(mesh):
    return jax.shard_map(
        per_device,
        mesh=mesh,
        in_specs=(
            P(("inline", "xline"), None),
            P(("inline", "xline"), None),
            P(("inline", "xline")),
            P(("inline", "xline")),
            P(),
            P(),
            P(),
        ),
        out_specs=P(None, "inline", "xline", None),
        check_vma=False,
    )
```

```python
import functools

import jax
import jax.numpy as jnp
from jax import lax
from jax.experimental import pallas as pl
from jax.experimental.pallas import tpu as pltpu
from jax.sharding import PartitionSpec as P

CLASSES = 8
BI = 2
BX = 2
GI = 2
LANES = 128
MESH = pl.DeviceIdType.MESH
F32 = jnp.float32
BF16 = jnp.bfloat16


def gelu(x):
    return 0.5 * x * (1.0 + jnp.tanh(0.7978845608028654 * (x + 0.044715 * (x * x * x))))


def split(value, size):
    if size & (size - 1):
        return lax.div(value, size), lax.rem(value, size)
    return value >> (size.bit_length() - 1), value & (size - 1)


def band_matrices(ch, XL, k1, k2, t1, t2):
    HR = ch * XL

    def banded(pieces, lane_x, x):
        low, mid, high = pieces
        zero = jnp.zeros_like(mid)
        return jnp.where(
            lane_x == x - 1, low, jnp.where(lane_x == x, mid, jnp.where(lane_x == x + 1, high, zero))
        )

    taps = [(di, dt) for di in range(3) for dt in range(3)]
    q1 = 9 * CLASSES
    lanes = lax.broadcasted_iota(jnp.int32, (q1, q1 * XL), 1)
    spread = jnp.where(
        split(lanes, XL)[0] == lax.broadcasted_iota(jnp.int32, (q1, q1 * XL), 0), 1.0, 0.0
    ).astype(BF16)
    pieces = []
    for dx in range(3):
        rows = jnp.concatenate([k1[di * 9 + dx * 3 + dt].astype(F32) for di, dt in taps], axis=0)
        pieces.append(
            lax.dot_general(
                rows.astype(BF16), spread, (((0,), (0,)), ((), ())), preferred_element_type=F32
            )
        )
    lane_x = split(lax.broadcasted_iota(jnp.int32, (ch, q1 * XL), 1), XL)[1]
    for x in range(XL):
        t1[x * ch:(x + 1) * ch, :] = banded(pieces, lane_x, x).astype(BF16)

    lane_x, lane_c = split(lax.broadcasted_iota(jnp.int32, (ch, HR), 1), ch)
    spread = jnp.where(lane_c == lax.broadcasted_iota(jnp.int32, (ch, HR), 0), 1.0, 0.0).astype(BF16)

    def tap(q, carry):
        first = (q // 3) * 9 + q % 3
        pieces = [jnp.dot(k2[first + dx * 3], spread, preferred_element_type=F32) for dx in range(3)]
        spot = pl.ds(pl.multiple_of(q * HR, LANES), HR)
        for x in range(XL):
            t2[x * ch:(x + 1) * ch, spot] = banded(pieces, lane_x, x).astype(BF16)
        return carry

    lax.fori_loop(0, 9, tap, 0)


def kernel(
    planes, xsize, rows, samples, ch,
    traces, target_h, bins_h, classes_h, band, k1_h, k2_h, out,
    target, bins, classes, k1, k2, codes, rx, crx, oh, own, counts, txz, rz, rl, ctx, crz, avg, anx, wts, vol, nxt, prv, low, high, v3, h3, t1, t2, outb,
    i_sem, w_sem, l_sem, o_sem, a_send, a_recv, c_send, c_recv, z_send, z_recv, l_recv, n_send, n_recv,
    e_send, e_recv, g_send, g_recv, y_send, y_recv,
):
    T = GI * xsize
    R = planes
    S = samples // T
    NCH = S // LANES
    I = GI * BI
    XL = xsize * BX
    CELLS = CLASSES * I * XL
    VR = CLASSES * XL
    HR = ch * XL
    inline = lax.axis_index("inline")
    xline = lax.axis_index("xline")
    z = lax.div(inline, GI)
    t = lax.rem(inline, GI) * xsize + xline

    def dev(zz, tt):
        return (zz * GI + lax.div(tt, xsize), lax.rem(tt, xsize))

    def mate(d):
        return lax.rem(t + d + T, T)

    def plane(d):
        return lax.rem(z + d + R, R)

    def remote(src, dst, ssem, rsem, target):
        return pltpu.make_async_remote_copy(
            src_ref=src, dst_ref=dst, send_sem=ssem, recv_sem=rsem,
            device_id=target, device_id_type=MESH,
        )

    weights = pltpu.make_async_copy(band.at[:, pl.ds(t * NCH, NCH)], wts, w_sem)
    local = []
    for c in range(NCH):
        col = pl.multiple_of(t * S + c * LANES, LANES)
        local.append(pltpu.make_async_copy(traces.at[:, pl.ds(col, LANES)], rx.at[c, 0], l_sem.at[c]))
    pairs = ((target_h, target), (bins_h, bins), (classes_h, classes), (k1_h, k1), (k2_h, k2))
    fetch = [pltpu.make_async_copy(a, b, i_sem.at[n]) for n, (a, b) in enumerate(pairs)]
    for copy in fetch:
        copy.start()

    barrier = pltpu.get_barrier_semaphore()
    partners = [dev(z, mate(d)) for d in range(1, T)]
    partners += [dev(plane(d), t) for d in range(1, R)]
    partners += [dev(plane(dz), mate(dt)) for dz in (-1, 1) for dt in (-1, 1)]
    for p in partners:
        pl.semaphore_signal(barrier, inc=1, device_id=p, device_id_type=MESH)

    for copy in fetch[:3]:
        copy.wait()
    dest_i, dest_x = split(target[...], xsize)
    dest_z, dest_a = split(dest_i, GI)
    bin_i, bin_x = split(bins[...], BX)
    code = dest_z * CELLS + (classes[...] * I + dest_a * BI + bin_i) * XL + dest_x * BX + bin_x
    codes[...] = jnp.broadcast_to(code, (8, rows))
    pl.semaphore_wait(barrier, len(partners))

    send_c, send_a = {}, {}
    for d in range(1, T):
        send_c[d] = remote(codes, crx.at[d], c_send.at[d], c_recv.at[d], dev(z, mate(d)))
        send_c[d].start()
    for c in range(NCH):
        for d in range(1, T):
            col = pl.multiple_of(mate(d) * S + c * LANES, LANES)
            send_a[c, d] = remote(
                traces.at[:, pl.ds(col, LANES)], rx.at[c, d],
                a_send.at[c * T + d], a_recv.at[c * T + d], dev(z, mate(d)),
            )
            send_a[c, d].start()
        local[c].start()
    weights.start()

    @pl.when(z == 0)
    def _():
        vol[0:2] = jnp.zeros((2,) + vol.shape[1:], BF16)
        nxt[0] = jnp.zeros(nxt.shape[1:], BF16)
        prv[0] = jnp.zeros(prv.shape[1:], BF16)

    @pl.when(z == R - 1)
    def _():
        vol[I + 2:I + 4] = jnp.zeros((2,) + vol.shape[1:], BF16)
        nxt[2] = jnp.zeros(nxt.shape[1:], BF16)
        prv[2] = jnp.zeros(prv.shape[1:], BF16)

    @pl.when(t == 0)
    def _():
        prv[...] = jnp.zeros(prv.shape, BF16)

    @pl.when(t == T - 1)
    def _():
        nxt[...] = jnp.zeros(nxt.shape, BF16)
        anx[...] = jnp.zeros(anx.shape, BF16)

    cell = lax.broadcasted_iota(jnp.int32, (CELLS, rows), 0)

    def one_hot(d, row):
        spot = pl.ds(pl.multiple_of(d * rows, LANES), rows)
        for r in range(R):
            oh[r, :, spot] = jnp.where(cell == row - r * CELLS, 1.0, 0.0).astype(BF16)

    def arrived_code(d, carry):
        remote(codes, crx.at[d], c_send.at[d], c_recv.at[d], dev(z, t)).wait_recv()
        one_hot(d, crx[d][0:1, :])
        return carry

    one_hot(0, codes[0:1, :])
    lax.fori_loop(1, T, arrived_code, 0)
    for copy in fetch[3:]:
        copy.wait()
    band_matrices(ch, XL, k1, k2, t1, t2)

    send_z, send_n = {}, {}
    outer = (z == 0) | (z == R - 1)

    def mirror(p):
        return jnp.where(z < 2, p, 3 - p)

    def hop(c, p, dst, rsem, r):
        return remote(txz.at[c, p], dst, z_send.at[c * R + p], rsem, dev(r, t))

    def hops(c):
        return {
            (0, True): hop(c, 0, rl.at[c], l_recv.at[c], mirror(1)),
            (0, False): hop(c, 0, rz.at[c, 0], z_recv.at[c * R], mirror(2)),
            (1, True): hop(c, 1, rz.at[c, 1], z_recv.at[c * R + 1], mirror(2)),
            (1, False): hop(c, 1, rz.at[c, 1], z_recv.at[c * R + 1], mirror(0)),
            (2, True): hop(c, 2, rz.at[c, 2], z_recv.at[c * R + 2], mirror(1)),
            (3, False): hop(c, 3, rz.at[c, 3], z_recv.at[c * R + 3], mirror(3)),
        }

    for c in range(NCH):
        local[c].wait()
        for d in range(1, T):
            send_a[c, d].wait_recv()
        data = rx[c].reshape(T * rows, LANES)
        data = jnp.concatenate([data, jnp.ones((T * rows, LANES), BF16)], axis=1)

        def summed(r):
            total = jnp.dot(oh[r], data, preferred_element_type=F32)
            if c == 0:
                counts[r] = total[:, LANES:]
            return total[:, :LANES]

        if R == 4:
            ways = hops(c)
            inner = jnp.logical_not(outer)

            def part(p, carry):
                r = mirror(jnp.where(outer, 3 - p, jnp.where(p == 0, 2, jnp.where(p == 3, 3, p - 1))))
                total = summed(r)
                txz[c, p] = total.astype(BF16)

                @pl.when((outer & (p == 3)) | (inner & (p == 2)))
                def _():
                    own[c] = total

                @pl.when(outer & (p == 0))
                def _():
                    ways[0, True].start()

                @pl.when(inner & (p == 0))
                def _():
                    ways[0, False].start()

                @pl.when(outer & (p == 1))
                def _():
                    ways[1, True].start()

                @pl.when(inner & (p == 1))
                def _():
                    ways[1, False].start()

                @pl.when(outer & (p == 2))
                def _():
                    ways[2, True].start()

                @pl.when(inner & (p == 3))
                def _():
                    ways[0, True].wait_recv()
                    txz[c, p] = (total + rl[c].astype(F32)).astype(BF16)
                    ways[3, False].start()

                return carry

            lax.fori_loop(0, 4, part, 0)
        else:
            for d in list(range(1, R)) + [0]:
                total = summed(plane(d))
                if d == 0:
                    own[c] = total
                else:
                    txz[c, d] = total.astype(BF16)
                    send_z[c, d] = hop(c, d, rz.at[c, d], z_recv.at[c * R + d], plane(d))
                    send_z[c, d].start()
        if c == 0:
            for d in range(1, R):
                ctx[d] = jnp.transpose(counts[plane(d)])[0:8]
                send_n[d] = remote(ctx.at[d], crz.at[d], n_send.at[d], n_recv.at[d], dev(plane(d), t))
                send_n[d].start()

    count = jnp.zeros((8, CELLS), F32)
    for d in range(1, R):
        send_n[d].wait_recv()
        count = count + crz[d]
    fold = counts[z] + jnp.transpose(jnp.broadcast_to(count[0:1], (LANES, CELLS)))
    fold = jnp.maximum(fold, 1.0)
    to_before = remote(avg.at[0], anx, e_send, e_recv, dev(z, mate(-1)))
    for c in range(NCH):
        if R == 4:
            ways = hops(c)

            @pl.when(outer)
            def _():
                ways[1, False].wait_recv()
                ways[3, False].wait_recv()
                own[c] = own[c] + rz[c, 1].astype(F32) + rz[c, 3].astype(F32)

            @pl.when(jnp.logical_not(outer))
            def _():
                for p in range(3):
                    ways[p, p == 2].wait_recv()
                own[c] = own[c] + rz[c, 0].astype(F32) + rz[c, 1].astype(F32) + rz[c, 2].astype(F32)

            total = own[c]
        else:
            total = own[c]
            for d in range(1, R):
                send_z[c, d].wait_recv()
                total = total + rz[c, d].astype(F32)
        avg[c] = (total / fold).astype(BF16)
        if c == 0:
            @pl.when(t > 0)
            def _():
                to_before.start()

    weights.wait()
    for k in range(NCH - 1):
        moveout(avg[k], avg[k + 1], wts, vol, k, I, XL)

    @pl.when(t < T - 1)
    def _():
        to_before.wait_recv()

    moveout(avg[NCH - 1], anx[...], wts, vol, NCH - 1, I, XL)

    pair = lax.broadcasted_iota(jnp.int32, (VR, LANES), 1) >> 1

    def turned(x, by):
        return pltpu.roll(x, by % LANES, 1) if by % LANES else x

    first_two = jnp.zeros((VR, LANES), F32)
    last_two = jnp.zeros((VR, LANES), F32)
    for i in range(I):
        begin = turned(vol[2 + i, :, 0:LANES].astype(F32), 2 * i)
        end = turned(vol[2 + i, :, S - LANES:S].astype(F32), -2 * i)
        first_two = jnp.where(pair == i, begin, first_two)
        last_two = jnp.where(pair == LANES // 2 - 1 - i, end, last_two)
    low[...] = first_two.astype(BF16)
    high[...] = last_two.astype(BF16)

    def border(dz, dt):
        here, there = {0: ((2, I), (2, I)), 1: ((I, 2), (0, 2)), -1: ((2, 2), (I + 2, 2))}[dz]
        src = vol.at[pl.ds(*here)]
        if dt == 0:
            dst = vol.at[pl.ds(*there)]
        elif dt == -1:
            src, dst = low.at[...], nxt.at[1 - dz]
        else:
            src, dst = high.at[...], prv.at[1 - dz]
        index = (dz + 1) * 3 + dt + 1
        return remote(src, dst, g_send.at[index], g_recv.at[index], dev(plane(dz), mate(dt)))

    def inside(dz, dt):
        return (z + dz >= 0) & (z + dz < R) & (t + dt >= 0) & (t + dt < T)

    sides = [(0, -1), (0, 1), (-1, 0), (1, 0), (-1, -1), (-1, 1), (1, -1), (1, 1)]
    for dz, dt in sides:
        @pl.when(inside(dz, dt))
        def _(dz=dz, dt=dt):
            border(dz, dt).start()

    def arrive(pairs):
        for dz, dt in pairs:
            @pl.when(inside(-dz, -dt))
            def _(dz=dz, dt=dt):
                border(dz, dt).wait_recv()

    width = S + LANES
    half = lax.broadcasted_iota(jnp.int32, (VR, LANES), 1) < LANES // 2
    lane = lax.broadcasted_iota(jnp.int32, (HR, width), 1)
    keep = (lane < S) | ((lane < S + LANES // 2) & (t < T - 1)) | ((lane >= S + LANES // 2) & (t > 0))

    def spread(r):
        source, i = (0, I - 2 + r) if r < 2 else (1, r - 2) if r < I + 2 else (2, r - I - 2)
        edge = jnp.where(
            half, turned(nxt[source].astype(F32), -2 * i), turned(prv[source].astype(F32), 2 * i)
        )
        full = jnp.concatenate([vol[r].astype(F32), edge], axis=1)
        v3[r, 0:VR] = pltpu.roll(full, 1, 1).astype(BF16)
        v3[r, VR:2 * VR] = full.astype(BF16)
        v3[r, 2 * VR:3 * VR] = pltpu.roll(full, width - 1, 1).astype(BF16)

    def first(r):
        total = jnp.dot(t1[...], v3[pl.ds(r, 3)].reshape(9 * VR, width), preferred_element_type=F32)
        real = ((r > 0) | (z > 0)) & ((r < I + 1) | (z < R - 1))
        value = jnp.where(keep & real, gelu(total), 0.0)
        h3[r, 0:HR] = pltpu.roll(value, 1, 1)[:, :S].astype(BF16)
        h3[r, HR:2 * HR] = value[:, :S].astype(BF16)
        h3[r, 2 * HR:3 * HR] = pltpu.roll(value, width - 1, 1)[:, :S].astype(BF16)

    arrive(sides[:2])
    for r in range(2, I + 2):
        spread(r)
    for r in range(2, I):
        first(r)
    arrive(sides[2:])
    for r in (0, 1, I + 2, I + 3):
        spread(r)

    mine = lax.div(t, xsize)

    def tile_row(phase, n):
        a = 1 - mine if phase == 0 else mine
        return a, a * BI + (1 - a) * (1 - n) + a * n

    def shared(phase, n, k):
        a, r = tile_row(phase, n)
        b = lax.rem(xline + k, xsize)
        source = outb.at[r, pl.ds(b * BX, BX)]
        spot = out.at[r - a * BI, :, :, pl.ds(pl.multiple_of(t * S, LANES), S)]
        index = (phase * BI + n) * xsize + k
        if phase == 1 and k == 0:
            return pltpu.make_async_copy(source, spot, o_sem.at[n])
        return remote(source, spot, y_send.at[index], y_recv.at[index], dev(z, a * xsize + b))

    def landed(phase, n, k):
        a = 1 - mine if phase == 0 else mine
        r = (1 - mine) * (1 - n) + mine * n
        b = lax.rem(xline - k + xsize, xsize)
        spot = out.at[r, :, :, pl.ds(pl.multiple_of((a * xsize + b) * S, LANES), S)]
        index = (phase * BI + n) * xsize + k
        source = outb.at[r, pl.ds(b * BX, BX)]
        return remote(source, spot, y_send.at[index], y_recv.at[index], dev(z, a * xsize + b))

    steps = [(phase, n) for phase in range(2) for n in range(BI)]
    for phase, n in steps:
        a, r = tile_row(phase, n)
        first(r + a * 2)
        total = jnp.dot(t2[...], h3[pl.ds(r, 3)].reshape(9 * HR, S), preferred_element_type=F32)
        outb[r] = total.astype(BF16).reshape(XL, ch, S)
        for k in range(xsize):
            shared(phase, n, k).start()
    for phase, n in steps:
        for k in range(xsize):
            if (phase, k) == (1, 0):
                shared(phase, n, k).wait()
            else:
                landed(phase, n, k).wait_recv()
                shared(phase, n, k).wait_send()

    for copy in (send_c, send_a, send_z, send_n):
        for item in copy.values():
            item.wait_send()
    if R == 4:
        for c in range(NCH):
            ways = hops(c)
            for p in range(2):
                ways[p, False].wait_send()

            @pl.when(outer)
            def _():
                ways[2, True].wait_send()

            @pl.when(jnp.logical_not(outer))
            def _():
                ways[3, False].wait_send()

    @pl.when(t > 0)
    def _():
        to_before.wait_send()

    for dz, dt in sides:
        @pl.when(inside(dz, dt))
        def _(dz=dz, dt=dt):
            border(dz, dt).wait_send()


def moveout(block, following, wts, vol, k, I, XL):
    bins = I * XL
    moved = []
    for c in range(CLASSES):
        both = jnp.concatenate(
            [block[c * bins:(c + 1) * bins], following[c * bins:(c + 1) * bins]], axis=1
        )
        moved.append(jnp.dot(both, wts[c, k], preferred_element_type=F32))
    for i in range(I):
        rows = jnp.concatenate([m[i * XL:(i + 1) * XL] for m in moved], axis=0)
        vol[2 + i, :, k * LANES:(k + 1) * LANES] = rows.astype(BF16)


def per_device(traces, trace_dest, trace_bin, trace_class, band_weights, conv_first, conv_second):
    inline_size = lax.axis_size("inline")
    xsize = lax.axis_size("xline")
    planes = inline_size // GI
    rows, samples = traces.shape
    ch = conv_first.shape[0]
    T = GI * xsize
    R = planes
    S = samples // T
    NCH = S // LANES
    I = GI * BI
    XL = xsize * BX
    CELLS = CLASSES * I * XL
    VR = CLASSES * XL
    HR = ch * XL
    nb, bw = band_weights.shape[1], band_weights.shape[-1]

    band = band_weights.reshape(CLASSES, nb, 2 * bw, bw)
    k1 = jnp.transpose(conv_first, (2, 3, 4, 1, 0)).reshape(27, CLASSES, ch)
    k2 = jnp.transpose(conv_second, (2, 3, 4, 0, 1)).reshape(27, ch, ch)

    hbm = pl.BlockSpec(memory_space=pltpu.HBM)
    dma = pltpu.SemaphoreType.DMA
    out = pl.pallas_call(
        functools.partial(kernel, planes, xsize, rows, samples, ch),
        out_shape=jax.ShapeDtypeStruct((BI, BX, ch, samples), BF16),
        in_specs=[hbm] * 7,
        out_specs=hbm,
        scratch_shapes=[
            pltpu.VMEM((1, rows), jnp.int32),
            pltpu.VMEM((1, rows), jnp.int32),
            pltpu.VMEM((1, rows), jnp.int32),
            pltpu.VMEM((27, CLASSES, ch), BF16),
            pltpu.VMEM((27, ch, ch), BF16),
            pltpu.VMEM((8, rows), jnp.int32),
            pltpu.VMEM((NCH, T, rows, LANES), BF16),
            pltpu.VMEM((T, 8, rows), jnp.int32),
            pltpu.VMEM((R, CELLS, T * rows), BF16),
            pltpu.VMEM((NCH, CELLS, LANES), F32),
            pltpu.VMEM((R, CELLS, LANES), F32),
            pltpu.VMEM((NCH, R, CELLS, LANES), BF16),
            pltpu.VMEM((NCH, R, CELLS, LANES), BF16),
            pltpu.VMEM((NCH, CELLS, LANES), BF16),
            pltpu.VMEM((R, 8, CELLS), F32),
            pltpu.VMEM((R, 8, CELLS), F32),
            pltpu.VMEM((NCH, CELLS, LANES), BF16),
            pltpu.VMEM((CELLS, LANES), BF16),
            pltpu.VMEM((CLASSES, NCH, 2 * bw, bw), BF16),
            pltpu.VMEM((I + 4, VR, S), BF16),
            pltpu.VMEM((3, VR, LANES), BF16),
            pltpu.VMEM((3, VR, LANES), BF16),
            pltpu.VMEM((VR, LANES), BF16),
            pltpu.VMEM((VR, LANES), BF16),
            pltpu.VMEM((I + 4, 3 * VR, S + LANES), BF16),
            pltpu.VMEM((I + 2, 3 * HR, S), BF16),
            pltpu.VMEM((HR, 9 * VR), BF16),
            pltpu.VMEM((HR, 9 * HR), BF16),
            pltpu.VMEM((I, XL, ch, S), BF16),
            dma((5,)), dma, dma((NCH,)), dma((BI,)),
            dma((NCH * T,)), dma((NCH * T,)),
            dma((T,)), dma((T,)),
            dma((NCH * R,)), dma((NCH * R,)), dma((NCH,)),
            dma((R,)), dma((R,)),
            dma, dma,
            dma((9,)), dma((9,)),
            dma((BI * T,)), dma((BI * T,)),
        ],
        compiler_params=pltpu.CompilerParams(
            collective_id=0, has_side_effects=True, vmem_limit_bytes=(61440 if T <= 8 else 60 * 1024) * 1024
        ),
        name="regularize",
    )(
        traces, trace_dest.reshape(1, rows), trace_bin.reshape(1, rows), trace_class.reshape(1, rows),
        band, k1, k2,
    )
    return jnp.transpose(out, (2, 0, 1, 3))


def solution(mesh):
    return jax.shard_map(
        per_device,
        mesh=mesh,
        in_specs=(
            P(("inline", "xline"), None),
            P(("inline", "xline"), None),
            P(("inline", "xline")),
            P(("inline", "xline")),
            P(),
            P(),
            P(),
        ),
        out_specs=P(None, "inline", "xline", None),
        check_vma=False,
    )
```

```python
import functools

import jax
import jax.numpy as jnp
from jax import lax
from jax.experimental import pallas as pl
from jax.experimental.pallas import tpu as pltpu
from jax.sharding import PartitionSpec as P

CLASSES = 8
BI = 2
BX = 2
GI = 2
LANES = 128
MESH = pl.DeviceIdType.MESH
F32 = jnp.float32
BF16 = jnp.bfloat16


def gelu(x):
    return 0.5 * x * (1.0 + jnp.tanh(0.7978845608028654 * (x + 0.044715 * (x * x * x))))


def split(value, size):
    if size & (size - 1):
        return lax.div(value, size), lax.rem(value, size)
    return value >> (size.bit_length() - 1), value & (size - 1)


def band_matrices(ch, XL, k1, k2, t1, t2):
    HR = ch * XL

    def banded(pieces, lane_x, x):
        low, mid, high = pieces
        zero = jnp.zeros_like(mid)
        return jnp.where(
            lane_x == x - 1, low, jnp.where(lane_x == x, mid, jnp.where(lane_x == x + 1, high, zero))
        )

    taps = [(di, dt) for di in range(3) for dt in range(3)]
    q1 = 9 * CLASSES
    lanes = lax.broadcasted_iota(jnp.int32, (q1, q1 * XL), 1)
    spread = jnp.where(
        split(lanes, XL)[0] == lax.broadcasted_iota(jnp.int32, (q1, q1 * XL), 0), 1.0, 0.0
    ).astype(BF16)
    pieces = []
    for dx in range(3):
        rows = jnp.concatenate([k1[di * 9 + dx * 3 + dt].astype(F32) for di, dt in taps], axis=0)
        pieces.append(
            lax.dot_general(
                rows.astype(BF16), spread, (((0,), (0,)), ((), ())), preferred_element_type=F32
            )
        )
    lane_x = split(lax.broadcasted_iota(jnp.int32, (ch, q1 * XL), 1), XL)[1]
    for x in range(XL):
        t1[x * ch:(x + 1) * ch, :] = banded(pieces, lane_x, x).astype(BF16)

    lane_x, lane_c = split(lax.broadcasted_iota(jnp.int32, (ch, HR), 1), ch)
    spread = jnp.where(lane_c == lax.broadcasted_iota(jnp.int32, (ch, HR), 0), 1.0, 0.0).astype(BF16)

    def tap(q, carry):
        first = (q // 3) * 9 + q % 3
        pieces = [jnp.dot(k2[first + dx * 3], spread, preferred_element_type=F32) for dx in range(3)]
        spot = pl.ds(pl.multiple_of(q * HR, LANES), HR)
        for x in range(XL):
            t2[x * ch:(x + 1) * ch, spot] = banded(pieces, lane_x, x).astype(BF16)
        return carry

    lax.fori_loop(0, 9, tap, 0)


def kernel(
    planes, xsize, rows, samples, ch,
    traces, target_h, bins_h, classes_h, band, k1_h, k2_h, out,
    target, bins, classes, k1, k2, codes, rx, crx, oh, own, counts, txz, rz, rl, ctx, crz, avg, anx, wts, vol, nxt, prv, low, high, v3, h3, t1, t2, outb,
    i_sem, w_sem, l_sem, o_sem, a_send, a_recv, c_send, c_recv, z_send, z_recv, l_recv, n_send, n_recv,
    e_send, e_recv, g_send, g_recv, y_send, y_recv,
):
    T = GI * xsize
    R = planes
    S = samples // T
    NCH = S // LANES
    I = GI * BI
    XL = xsize * BX
    CELLS = CLASSES * I * XL
    VR = CLASSES * XL
    HR = ch * XL
    inline = lax.axis_index("inline")
    xline = lax.axis_index("xline")
    z = lax.div(inline, GI)
    t = lax.rem(inline, GI) * xsize + xline

    def dev(zz, tt):
        return (zz * GI + lax.div(tt, xsize), lax.rem(tt, xsize))

    def mate(d):
        return lax.rem(t + d + T, T)

    def plane(d):
        return lax.rem(z + d + R, R)

    def remote(src, dst, ssem, rsem, target):
        return pltpu.make_async_remote_copy(
            src_ref=src, dst_ref=dst, send_sem=ssem, recv_sem=rsem,
            device_id=target, device_id_type=MESH,
        )

    weights = pltpu.make_async_copy(band.at[:, pl.ds(t * NCH, NCH)], wts, w_sem)
    local = []
    for c in range(NCH):
        col = pl.multiple_of(t * S + c * LANES, LANES)
        local.append(pltpu.make_async_copy(traces.at[:, pl.ds(col, LANES)], rx.at[c, 0], l_sem.at[c]))
    pairs = ((target_h, target), (bins_h, bins), (classes_h, classes), (k1_h, k1), (k2_h, k2))
    fetch = [pltpu.make_async_copy(a, b, i_sem.at[n]) for n, (a, b) in enumerate(pairs)]
    for copy in fetch:
        copy.start()

    barrier = pltpu.get_barrier_semaphore()
    partners = [dev(z, mate(d)) for d in range(1, T)]
    partners += [dev(plane(d), t) for d in range(1, R)]
    partners += [dev(plane(dz), mate(dt)) for dz in (-1, 1) for dt in (-1, 1)]
    for p in partners:
        pl.semaphore_signal(barrier, inc=1, device_id=p, device_id_type=MESH)

    for copy in fetch[:3]:
        copy.wait()
    dest_i, dest_x = split(target[...], xsize)
    dest_z, dest_a = split(dest_i, GI)
    bin_i, bin_x = split(bins[...], BX)
    code = dest_z * CELLS + (classes[...] * I + dest_a * BI + bin_i) * XL + dest_x * BX + bin_x
    codes[...] = jnp.broadcast_to(code, (8, rows))
    pl.semaphore_wait(barrier, len(partners))

    send_c, send_a = {}, {}
    for d in range(1, T):
        send_c[d] = remote(codes, crx.at[d], c_send.at[d], c_recv.at[d], dev(z, mate(d)))
        send_c[d].start()
    far_first = sorted(range(1, T), key=lambda d: abs(d - T // 2))

    def send_chunk(c):
        for d in far_first:
            col = pl.multiple_of(mate(d) * S + c * LANES, LANES)
            send_a[c, d] = remote(
                traces.at[:, pl.ds(col, LANES)], rx.at[c, d],
                a_send.at[c * T + d], a_recv.at[c * T + d], dev(z, mate(d)),
            )
            send_a[c, d].start()
        local[c].start()

    send_chunk(0)
    weights.start()

    @pl.when(z == 0)
    def _():
        vol[0:2] = jnp.zeros((2,) + vol.shape[1:], BF16)
        nxt[0] = jnp.zeros(nxt.shape[1:], BF16)
        prv[0] = jnp.zeros(prv.shape[1:], BF16)

    @pl.when(z == R - 1)
    def _():
        vol[I + 2:I + 4] = jnp.zeros((2,) + vol.shape[1:], BF16)
        nxt[2] = jnp.zeros(nxt.shape[1:], BF16)
        prv[2] = jnp.zeros(prv.shape[1:], BF16)

    @pl.when(t == 0)
    def _():
        prv[...] = jnp.zeros(prv.shape, BF16)

    @pl.when(t == T - 1)
    def _():
        nxt[...] = jnp.zeros(nxt.shape, BF16)
        anx[...] = jnp.zeros(anx.shape, BF16)

    cell = lax.broadcasted_iota(jnp.int32, (CELLS, rows), 0)

    def one_hot(d, row):
        spot = pl.ds(pl.multiple_of(d * rows, LANES), rows)
        for r in range(R):
            oh[r, :, spot] = jnp.where(cell == row - r * CELLS, 1.0, 0.0).astype(BF16)

    def arrived_code(d, carry):
        remote(codes, crx.at[d], c_send.at[d], c_recv.at[d], dev(z, t)).wait_recv()
        one_hot(d, crx[d][0:1, :])
        return carry

    one_hot(0, codes[0:1, :])
    lax.fori_loop(1, T, arrived_code, 0)
    for c in range(1, NCH):
        send_chunk(c)
    for copy in fetch[3:]:
        copy.wait()
    band_matrices(ch, XL, k1, k2, t1, t2)

    send_z, send_n = {}, {}
    outer = (z == 0) | (z == R - 1)

    def mirror(p):
        return jnp.where(z < 2, p, 3 - p)

    def hop(c, p, dst, rsem, r):
        return remote(txz.at[c, p], dst, z_send.at[c * R + p], rsem, dev(r, t))

    def hops(c):
        return {
            (0, True): hop(c, 0, rl.at[c], l_recv.at[c], mirror(1)),
            (0, False): hop(c, 0, rz.at[c, 0], z_recv.at[c * R], mirror(2)),
            (1, True): hop(c, 1, rz.at[c, 1], z_recv.at[c * R + 1], mirror(2)),
            (1, False): hop(c, 1, rz.at[c, 1], z_recv.at[c * R + 1], mirror(0)),
            (2, True): hop(c, 2, rz.at[c, 2], z_recv.at[c * R + 2], mirror(1)),
            (3, False): hop(c, 3, rz.at[c, 3], z_recv.at[c * R + 3], mirror(3)),
        }

    for c in range(NCH):
        local[c].wait()
        for d in range(1, T):
            send_a[c, d].wait_recv()
        data = rx[c].reshape(T * rows, LANES)
        data = jnp.concatenate([data, jnp.ones((T * rows, LANES), BF16)], axis=1)

        def summed(r):
            total = jnp.dot(oh[r], data, preferred_element_type=F32)
            if c == 0:
                counts[r] = total[:, LANES:]
            return total[:, :LANES]

        if R == 4:
            ways = hops(c)
            inner = jnp.logical_not(outer)

            def part(p, carry):
                r = mirror(jnp.where(outer, 3 - p, jnp.where(p == 0, 2, jnp.where(p == 3, 3, p - 1))))
                total = summed(r)
                txz[c, p] = total.astype(BF16)

                @pl.when((outer & (p == 3)) | (inner & (p == 2)))
                def _():
                    own[c] = total

                @pl.when(outer & (p == 0))
                def _():
                    ways[0, True].start()

                @pl.when(inner & (p == 0))
                def _():
                    ways[0, False].start()

                @pl.when(outer & (p == 1))
                def _():
                    ways[1, True].start()

                @pl.when(inner & (p == 1))
                def _():
                    ways[1, False].start()

                @pl.when(outer & (p == 2))
                def _():
                    ways[2, True].start()

                @pl.when(inner & (p == 3))
                def _():
                    ways[0, True].wait_recv()
                    txz[c, p] = (total + rl[c].astype(F32)).astype(BF16)
                    ways[3, False].start()

                return carry

            lax.fori_loop(0, 4, part, 0)
        else:
            for d in list(range(1, R)) + [0]:
                total = summed(plane(d))
                if d == 0:
                    own[c] = total
                else:
                    txz[c, d] = total.astype(BF16)
                    send_z[c, d] = hop(c, d, rz.at[c, d], z_recv.at[c * R + d], plane(d))
                    send_z[c, d].start()
        if c == 0:
            for d in range(1, R):
                ctx[d] = jnp.transpose(counts[plane(d)])[0:8]
                send_n[d] = remote(ctx.at[d], crz.at[d], n_send.at[d], n_recv.at[d], dev(plane(d), t))
                send_n[d].start()

    count = jnp.zeros((8, CELLS), F32)
    for d in range(1, R):
        send_n[d].wait_recv()
        count = count + crz[d]
    fold = counts[z] + jnp.transpose(jnp.broadcast_to(count[0:1], (LANES, CELLS)))
    fold = jnp.maximum(fold, 1.0)
    to_before = remote(avg.at[0], anx, e_send, e_recv, dev(z, mate(-1)))
    for c in range(NCH):
        if R == 4:
            ways = hops(c)

            @pl.when(outer)
            def _():
                ways[1, False].wait_recv()
                ways[3, False].wait_recv()
                own[c] = own[c] + rz[c, 1].astype(F32) + rz[c, 3].astype(F32)

            @pl.when(jnp.logical_not(outer))
            def _():
                for p in range(3):
                    ways[p, p == 2].wait_recv()
                own[c] = own[c] + rz[c, 0].astype(F32) + rz[c, 1].astype(F32) + rz[c, 2].astype(F32)

            total = own[c]
        else:
            total = own[c]
            for d in range(1, R):
                send_z[c, d].wait_recv()
                total = total + rz[c, d].astype(F32)
        avg[c] = (total / fold).astype(BF16)
        if c == 0:
            @pl.when(t > 0)
            def _():
                to_before.start()

    weights.wait()
    for k in range(NCH - 1):
        moveout(avg[k], avg[k + 1], wts, vol, k, I, XL)

    @pl.when(t < T - 1)
    def _():
        to_before.wait_recv()

    moveout(avg[NCH - 1], anx[...], wts, vol, NCH - 1, I, XL)

    pair = lax.broadcasted_iota(jnp.int32, (VR, LANES), 1) >> 1

    def turned(x, by):
        return pltpu.roll(x, by % LANES, 1) if by % LANES else x

    first_two = jnp.zeros((VR, LANES), F32)
    last_two = jnp.zeros((VR, LANES), F32)
    for i in range(I):
        begin = turned(vol[2 + i, :, 0:LANES].astype(F32), 2 * i)
        end = turned(vol[2 + i, :, S - LANES:S].astype(F32), -2 * i)
        first_two = jnp.where(pair == i, begin, first_two)
        last_two = jnp.where(pair == LANES // 2 - 1 - i, end, last_two)
    low[...] = first_two.astype(BF16)
    high[...] = last_two.astype(BF16)

    def border(dz, dt):
        here, there = {0: ((2, I), (2, I)), 1: ((I, 2), (0, 2)), -1: ((2, 2), (I + 2, 2))}[dz]
        src = vol.at[pl.ds(*here)]
        if dt == 0:
            dst = vol.at[pl.ds(*there)]
        elif dt == -1:
            src, dst = low.at[...], nxt.at[1 - dz]
        else:
            src, dst = high.at[...], prv.at[1 - dz]
        index = (dz + 1) * 3 + dt + 1
        return remote(src, dst, g_send.at[index], g_recv.at[index], dev(plane(dz), mate(dt)))

    def inside(dz, dt):
        return (z + dz >= 0) & (z + dz < R) & (t + dt >= 0) & (t + dt < T)

    sides = [(0, -1), (0, 1), (-1, 0), (1, 0), (-1, -1), (-1, 1), (1, -1), (1, 1)]
    for dz, dt in sides:
        @pl.when(inside(dz, dt))
        def _(dz=dz, dt=dt):
            border(dz, dt).start()

    def arrive(pairs):
        for dz, dt in pairs:
            @pl.when(inside(-dz, -dt))
            def _(dz=dz, dt=dt):
                border(dz, dt).wait_recv()

    width = S + LANES
    half = lax.broadcasted_iota(jnp.int32, (VR, LANES), 1) < LANES // 2
    lane = lax.broadcasted_iota(jnp.int32, (HR, width), 1)
    keep = (lane < S) | ((lane < S + LANES // 2) & (t < T - 1)) | ((lane >= S + LANES // 2) & (t > 0))

    def spread(r):
        source, i = (0, I - 2 + r) if r < 2 else (1, r - 2) if r < I + 2 else (2, r - I - 2)
        edge = jnp.where(
            half, turned(nxt[source].astype(F32), -2 * i), turned(prv[source].astype(F32), 2 * i)
        )
        full = jnp.concatenate([vol[r].astype(F32), edge], axis=1)
        v3[r, 0:VR] = pltpu.roll(full, 1, 1).astype(BF16)
        v3[r, VR:2 * VR] = full.astype(BF16)
        v3[r, 2 * VR:3 * VR] = pltpu.roll(full, width - 1, 1).astype(BF16)

    def first(r):
        total = jnp.dot(t1[...], v3[pl.ds(r, 3)].reshape(9 * VR, width), preferred_element_type=F32)
        real = ((r > 0) | (z > 0)) & ((r < I + 1) | (z < R - 1))
        value = jnp.where(keep & real, gelu(total), 0.0)
        h3[r, 0:HR] = pltpu.roll(value, 1, 1)[:, :S].astype(BF16)
        h3[r, HR:2 * HR] = value[:, :S].astype(BF16)
        h3[r, 2 * HR:3 * HR] = pltpu.roll(value, width - 1, 1)[:, :S].astype(BF16)

    arrive(sides[:2])
    for r in range(2, I + 2):
        spread(r)
    for r in range(2, I):
        first(r)
    arrive(sides[2:])
    for r in (0, 1, I + 2, I + 3):
        spread(r)

    mine = lax.div(t, xsize)

    def tile_row(phase, n):
        a = 1 - mine if phase == 0 else mine
        return a, a * BI + (1 - a) * (1 - n) + a * n

    def shared(phase, n, k):
        a, r = tile_row(phase, n)
        b = lax.rem(xline + k, xsize)
        source = outb.at[r, pl.ds(b * BX, BX)]
        spot = out.at[r - a * BI, :, :, pl.ds(pl.multiple_of(t * S, LANES), S)]
        index = (phase * BI + n) * xsize + k
        if phase == 1 and k == 0:
            return pltpu.make_async_copy(source, spot, o_sem.at[n])
        return remote(source, spot, y_send.at[index], y_recv.at[index], dev(z, a * xsize + b))

    def landed(phase, n, k):
        a = 1 - mine if phase == 0 else mine
        r = (1 - mine) * (1 - n) + mine * n
        b = lax.rem(xline - k + xsize, xsize)
        spot = out.at[r, :, :, pl.ds(pl.multiple_of((a * xsize + b) * S, LANES), S)]
        index = (phase * BI + n) * xsize + k
        source = outb.at[r, pl.ds(b * BX, BX)]
        return remote(source, spot, y_send.at[index], y_recv.at[index], dev(z, a * xsize + b))

    steps = [(phase, n) for phase in range(2) for n in range(BI)]
    for phase, n in steps:
        a, r = tile_row(phase, n)
        first(r + a * 2)
        total = jnp.dot(t2[...], h3[pl.ds(r, 3)].reshape(9 * HR, S), preferred_element_type=F32)
        outb[r] = total.astype(BF16).reshape(XL, ch, S)
        for k in range(xsize):
            shared(phase, n, k).start()
    for phase, n in steps:
        for k in range(xsize):
            if (phase, k) == (1, 0):
                shared(phase, n, k).wait()
            else:
                landed(phase, n, k).wait_recv()
                shared(phase, n, k).wait_send()

    for copy in (send_c, send_a, send_z, send_n):
        for item in copy.values():
            item.wait_send()
    if R == 4:
        for c in range(NCH):
            ways = hops(c)
            for p in range(2):
                ways[p, False].wait_send()

            @pl.when(outer)
            def _():
                ways[2, True].wait_send()

            @pl.when(jnp.logical_not(outer))
            def _():
                ways[3, False].wait_send()

    @pl.when(t > 0)
    def _():
        to_before.wait_send()

    for dz, dt in sides:
        @pl.when(inside(dz, dt))
        def _(dz=dz, dt=dt):
            border(dz, dt).wait_send()


def moveout(block, following, wts, vol, k, I, XL):
    bins = I * XL
    moved = []
    for c in range(CLASSES):
        both = jnp.concatenate(
            [block[c * bins:(c + 1) * bins], following[c * bins:(c + 1) * bins]], axis=1
        )
        moved.append(jnp.dot(both, wts[c, k], preferred_element_type=F32))
    for i in range(I):
        rows = jnp.concatenate([m[i * XL:(i + 1) * XL] for m in moved], axis=0)
        vol[2 + i, :, k * LANES:(k + 1) * LANES] = rows.astype(BF16)


def per_device(traces, trace_dest, trace_bin, trace_class, band_weights, conv_first, conv_second):
    inline_size = lax.axis_size("inline")
    xsize = lax.axis_size("xline")
    planes = inline_size // GI
    rows, samples = traces.shape
    ch = conv_first.shape[0]
    T = GI * xsize
    R = planes
    S = samples // T
    NCH = S // LANES
    I = GI * BI
    XL = xsize * BX
    CELLS = CLASSES * I * XL
    VR = CLASSES * XL
    HR = ch * XL
    nb, bw = band_weights.shape[1], band_weights.shape[-1]

    band = band_weights.reshape(CLASSES, nb, 2 * bw, bw)
    k1 = jnp.transpose(conv_first, (2, 3, 4, 1, 0)).reshape(27, CLASSES, ch)
    k2 = jnp.transpose(conv_second, (2, 3, 4, 0, 1)).reshape(27, ch, ch)

    hbm = pl.BlockSpec(memory_space=pltpu.HBM)
    dma = pltpu.SemaphoreType.DMA
    out = pl.pallas_call(
        functools.partial(kernel, planes, xsize, rows, samples, ch),
        out_shape=jax.ShapeDtypeStruct((BI, BX, ch, samples), BF16),
        in_specs=[hbm] * 7,
        out_specs=hbm,
        scratch_shapes=[
            pltpu.VMEM((1, rows), jnp.int32),
            pltpu.VMEM((1, rows), jnp.int32),
            pltpu.VMEM((1, rows), jnp.int32),
            pltpu.VMEM((27, CLASSES, ch), BF16),
            pltpu.VMEM((27, ch, ch), BF16),
            pltpu.VMEM((8, rows), jnp.int32),
            pltpu.VMEM((NCH, T, rows, LANES), BF16),
            pltpu.VMEM((T, 8, rows), jnp.int32),
            pltpu.VMEM((R, CELLS, T * rows), BF16),
            pltpu.VMEM((NCH, CELLS, LANES), F32),
            pltpu.VMEM((R, CELLS, LANES), F32),
            pltpu.VMEM((NCH, R, CELLS, LANES), BF16),
            pltpu.VMEM((NCH, R, CELLS, LANES), BF16),
            pltpu.VMEM((NCH, CELLS, LANES), BF16),
            pltpu.VMEM((R, 8, CELLS), F32),
            pltpu.VMEM((R, 8, CELLS), F32),
            pltpu.VMEM((NCH, CELLS, LANES), BF16),
            pltpu.VMEM((CELLS, LANES), BF16),
            pltpu.VMEM((CLASSES, NCH, 2 * bw, bw), BF16),
            pltpu.VMEM((I + 4, VR, S), BF16),
            pltpu.VMEM((3, VR, LANES), BF16),
            pltpu.VMEM((3, VR, LANES), BF16),
            pltpu.VMEM((VR, LANES), BF16),
            pltpu.VMEM((VR, LANES), BF16),
            pltpu.VMEM((I + 4, 3 * VR, S + LANES), BF16),
            pltpu.VMEM((I + 2, 3 * HR, S), BF16),
            pltpu.VMEM((HR, 9 * VR), BF16),
            pltpu.VMEM((HR, 9 * HR), BF16),
            pltpu.VMEM((I, XL, ch, S), BF16),
            dma((5,)), dma, dma((NCH,)), dma((BI,)),
            dma((NCH * T,)), dma((NCH * T,)),
            dma((T,)), dma((T,)),
            dma((NCH * R,)), dma((NCH * R,)), dma((NCH,)),
            dma((R,)), dma((R,)),
            dma, dma,
            dma((9,)), dma((9,)),
            dma((BI * T,)), dma((BI * T,)),
        ],
        compiler_params=pltpu.CompilerParams(
            collective_id=0, has_side_effects=True, vmem_limit_bytes=(61440 if T <= 8 else 60 * 1024) * 1024
        ),
        name="regularize",
    )(
        traces, trace_dest.reshape(1, rows), trace_bin.reshape(1, rows), trace_class.reshape(1, rows),
        band, k1, k2,
    )
    return jnp.transpose(out, (2, 0, 1, 3))


def solution(mesh):
    return jax.shard_map(
        per_device,
        mesh=mesh,
        in_specs=(
            P(("inline", "xline"), None),
            P(("inline", "xline"), None),
            P(("inline", "xline")),
            P(("inline", "xline")),
            P(),
            P(),
            P(),
        ),
        out_specs=P(None, "inline", "xline", None),
        check_vma=False,
    )
```
